128 devices in a mesh: gx: 8 (over y, x_lo), gy: 16 (over z, x_hi, core).
Axes of the slice: x: 4 (x_hi: 2, x_lo: 2; x = x_hi * 2 + x_lo), y: 4, z: 4, core: 2. Of those that a mesh axis runs over, the one named last changes fastest.
Arguments:
- dist_start: float32 [19, 2, 1024, 2048], P(None, None, 'gx', 'gy'), may hold values from -6 to 6
- cotangent: float32 [19, 2, 1024, 2048], P(None, None, 'gx', 'gy'), may hold values from -6 to 6
- solid_mask: int32 [2, 1024, 2048], P(None, 'gx', 'gy'), may hold values 0 or 1
- weight_in: bfloat16 [19, 128], replicated, may hold values from -1.25 to 1.25
- bias_in: float32 [128], replicated, may hold values from -3 to 3
- weight_out: bfloat16 [128, 19], replicated, may hold values from -0.5 to 0.5
- bias_out: float32 [19], replicated, may hold values from -3 to 3
Outputs:
- grad_start: float32 [19, 2, 1024, 2048], P(None, None, 'gx', 'gy')
- grad_weight_in: float32 [19, 128], replicated
- grad_bias_in: float32 [128], replicated
- grad_weight_out: float32 [128, 19], replicated
- grad_bias_out: float32 [19], replicated
The draws below stay inside these ranges and needn't reach their ends.
Inputs may be any that keep to these rules, and one draw needn't show every extreme that they name: `solid_mask`: 1 marks a solid cell.
All inputs are finite; a program needn't handle non-finite values. No bound on the sum of `solid_mask` on one device may be relied on, other than what follows from the above.
Results may differ from the reference program's by a relative error of at most 0.0067.
Values may be sent and summed in bfloat16 or wider, within the bound.
No kernel may reach another device: no remote copies, remote signals or barrier semaphores. Data moves between devices by JAX's collectives and lax.ppermute only.
A program may use at most 256 MiB of HBM per device.

```python
import math
import jax
import jax.numpy as jnp
import numpy as np
from jax import lax

Q = 19
H = 128
NZ = 2
NX = 1024
NY = 2048
CELLS = 4194304


def plant(values, rng, low, top_value):
    place = [jax.random.randint(jax.random.fold_in(rng, axis), (), 0, length) for axis, length in enumerate(values.shape)]
    widest = values.shape.index(max(values.shape))
    next_to = place[:widest] + [(place[widest] + 1) % values.shape[widest]] + place[widest + 1:]
    return values.at[tuple(place)].set(low).at[tuple(next_to)].set(top_value)


def steps_of(stream_key, shape, split, least, high):
    factor_of = 1.0
    for dim, blocks in split:
        draws = jax.random.uniform(jax.random.fold_in(jax.random.fold_in(stream_key, 6), dim), (blocks,), jnp.float32, least / len(split), high / len(split))
        factor_of = factor_of * jnp.repeat(jnp.exp(draws), shape[dim] // blocks).reshape((-1,) + (1,) * (len(shape) - 1 - dim))
    return factor_of


def bell_draw(own_key, dims, spread, bound, cuts=(), kind=jnp.bfloat16):
    values = spread * jax.random.normal(own_key, dims, jnp.float32)
    if cuts:
        values = values * steps_of(own_key, dims, cuts, -0.22, 0.18)
    return jnp.clip(values, -bound, bound).astype(kind)


def setup_inputs(seed: int = 0) -> dict:
    arg_keys = jax.random.split(jax.random.key(seed), 8)
    dist_start = bell_draw(arg_keys[0], (Q, NZ, NX, NY), 1.0, 6.0, ((2, 8), (3, 16)), jnp.float32)
    cotangent = bell_draw(arg_keys[1], (Q, NZ, NX, NY), 1.0, 6.0, ((2, 8), (3, 16)), jnp.float32)
    solid_mask = plant((jax.random.randint(arg_keys[2], (NZ, NX, NY), 0, 4) < 1).astype(jnp.int32), jax.random.fold_in(arg_keys[2], 1), 0, 1)
    weight_in = bell_draw(arg_keys[3], (Q, H), Q ** -0.5, 1.25)
    bias_in = bell_draw(arg_keys[4], (H,), 0.5, 3.0, (), jnp.float32)
    weight_out = bell_draw(arg_keys[5], (H, Q), H ** -0.5, 0.5)
    bias_out = bell_draw(arg_keys[6], (Q,), 0.5, 3.0, (), jnp.float32)
    return {"dist_start": dist_start, "cotangent": cotangent, "solid_mask": solid_mask, "weight_in": weight_in, "bias_in": bias_in, "weight_out": weight_out, "bias_out": bias_out}


velocities = ((0, 0, 0), (1, 0, 0), (-1, 0, 0), (0, 1, 0), (0, -1, 0), (0, 0, 1), (0, 0, -1), (1, 1, 0), (-1, -1, 0), (1, -1, 0), (-1, 1, 0), (1, 0, 1), (-1, 0, -1), (1, 0, -1), (-1, 0, 1), (0, 1, 1), (0, -1, -1), (0, 1, -1), (0, -1, 1))
opposite = (0, 2, 1, 4, 3, 6, 5, 8, 7, 10, 9, 12, 11, 14, 13, 16, 15, 18, 17)

def stream(density, orient):
    pieces = []
    for component in range(19):
        move_x, move_y, move_z = velocities[component]
        pieces.append(jnp.roll(density[component], (orient * move_z, orient * move_x, orient * move_y), axis=(0, 1, 2)))
    return jnp.stack(pieces)

def hidden_of(flat_bf, weight_in, bias_in):
    preact = jnp.einsum('qh,qc->hc', weight_in.astype(jnp.float32), flat_bf.astype(jnp.float32)) + bias_in[:, None]
    return jnp.tanh(preact)

def collide_block(flat_cells, solid_flat, weight_in, bias_in, weight_out, bias_out):
    flat_bf = lax.optimization_barrier(flat_cells.astype(jnp.bfloat16))
    active = lax.optimization_barrier(hidden_of(flat_bf, weight_in, bias_in).astype(jnp.bfloat16))
    output = jnp.einsum('hq,hc->qc', weight_out.astype(jnp.float32), active.astype(jnp.float32)) + bias_out[:, None]
    bounced = flat_cells[np.array(opposite)]
    return jnp.where(solid_flat[None, :] > 0, bounced, flat_cells + output)

def backward_block(flat_cells, solid_flat, grad_post, weight_in, bias_in, weight_out):
    flat_bf = lax.optimization_barrier(flat_cells.astype(jnp.bfloat16))
    tanh_val = hidden_of(flat_bf, weight_in, bias_in)
    active = lax.optimization_barrier(tanh_val.astype(jnp.bfloat16))
    is_solid = solid_flat[None, :] > 0
    out_grad = jnp.where(is_solid, jnp.float32(0.0), grad_post)
    out_bf = lax.optimization_barrier(out_grad.astype(jnp.bfloat16))
    hid_grad = jnp.einsum('hq,qc->hc', weight_out.astype(jnp.float32), out_bf.astype(jnp.float32)) * (1.0 - tanh_val * tanh_val)
    hid_bf = lax.optimization_barrier(hid_grad.astype(jnp.bfloat16))
    in_grad = out_grad + jnp.einsum('qh,hc->qc', weight_in.astype(jnp.float32), hid_bf.astype(jnp.float32))
    in_grad = in_grad + jnp.where(is_solid, grad_post[np.array(opposite)], jnp.float32(0.0))
    d_weight_in = jnp.einsum('qc,hc->qh', flat_bf.astype(jnp.float32), hid_bf.astype(jnp.float32))
    d_bias_in = lax.optimization_barrier(jnp.sum(hid_grad, axis=1))
    d_weight_out = jnp.einsum('hc,qc->hq', active.astype(jnp.float32), out_bf.astype(jnp.float32))
    d_bias_out = lax.optimization_barrier(jnp.sum(out_grad, axis=1))
    return (in_grad, (d_weight_in, d_bias_in, d_weight_out, d_bias_out))

def to_blocks(flat_cells, block):
    return jnp.transpose(flat_cells.reshape(flat_cells.shape[0], -1, block), (1, 0, 2))

def from_blocks(blocks):
    return jnp.transpose(blocks, (1, 0, 2)).reshape(blocks.shape[1], -1)

def collide(density, solid_mask, weight_in, bias_in, weight_out, bias_out):
    total = solid_mask.size
    block = math.gcd(total, 65536)
    flat_blocks = to_blocks(density.reshape(density.shape[0], -1), block)
    solid_blocks = solid_mask.reshape(-1, block)

    def one_block(pair):
        return collide_block(pair[0], pair[1], weight_in, bias_in, weight_out, bias_out)
    posts = lax.map(one_block, (flat_blocks, solid_blocks))
    return from_blocks(posts).reshape(density.shape)

def backward(density, solid_mask, grad_post, weight_in, bias_in, weight_out):
    total = solid_mask.size
    block = math.gcd(total, 65536)
    flat_blocks = to_blocks(density.reshape(density.shape[0], -1), block)
    grad_blocks = to_blocks(grad_post.reshape(grad_post.shape[0], -1), block)
    solid_blocks = solid_mask.reshape(-1, block)
    number = density.shape[0]
    hidden = weight_in.shape[1]
    start = (jnp.zeros((number, hidden), jnp.float32), jnp.zeros((hidden,), jnp.float32), jnp.zeros((hidden, number), jnp.float32), jnp.zeros((number,), jnp.float32))

    def one_block(carry, triple):
        in_grad, parts = backward_block(triple[0], triple[1], triple[2], weight_in, bias_in, weight_out)
        return (tuple((carry[i] + parts[i] for i in range(4))), in_grad)
    totals, in_grads = lax.scan(one_block, start, (flat_blocks, solid_blocks, grad_blocks))
    return (from_blocks(in_grads).reshape(density.shape), totals)

def reference(dist_start, cotangent, solid_mask, weight_in, bias_in, weight_out, bias_out):
    post_start = collide(dist_start, solid_mask, weight_in, bias_in, weight_out, bias_out).astype(jnp.bfloat16)
    dist_middle = stream(post_start, 1)
    grad_post_middle = stream(cotangent, -1)
    grad_middle, partials_late = backward(dist_middle, solid_mask, grad_post_middle, weight_in, bias_in, weight_out)
    grad_post_start = stream(grad_middle, -1)
    grad_start, partials_early = backward(dist_start, solid_mask, grad_post_start, weight_in, bias_in, weight_out)
    factor = 1.0 / math.sqrt(CELLS)
    return (grad_start, (partials_early[0] + partials_late[0]) * factor, (partials_early[1] + partials_late[1]) * factor, (partials_early[2] + partials_late[2]) * factor, (partials_early[3] + partials_late[3]) * factor)
```

```python
import math

import jax
import jax.numpy as jnp
from jax import lax
from jax.experimental import pallas as pl
from jax.experimental.pallas import tpu as pltpu
from jax.sharding import PartitionSpec as P

VEL = (
    (0, 0, 0), (1, 0, 0), (-1, 0, 0), (0, 1, 0), (0, -1, 0), (0, 0, 1), (0, 0, -1),
    (1, 1, 0), (-1, -1, 0), (1, -1, 0), (-1, 1, 0), (1, 0, 1), (-1, 0, -1), (1, 0, -1),
    (-1, 0, 1), (0, 1, 1), (0, -1, -1), (0, 1, -1), (0, -1, 1),
)
OPP = (0, 2, 1, 4, 3, 6, 5, 8, 7, 10, 9, 12, 11, 14, 13, 16, 15, 18, 17)
Q = 19
SIDE = tuple(q for q in range(Q) if VEL[q][1])
PLACE = {q: i for i, q in enumerate(SIDE)}
f32 = jnp.float32
bf16 = jnp.bfloat16
NT = (((1,), (1,)), ((), ()))
IDX = 80
COLS = (126, 127, 0, 0, 127, 127, 0, 1)


def iota(shape, dim):
    return lax.broadcasted_iota(jnp.int32, shape, dim)


def vmem(n):
    return [pl.BlockSpec(memory_space=pltpu.VMEM)] * n


def weights_kernel(wint, wout, wtin, wtout, bias, a_in, a_out, b_out, b_in):
    rep = jnp.where(iota((Q, 160), 1) // 8 == iota((Q, 160), 0), 1.0, 0.0).astype(bf16)
    rept = jnp.where(iota((160, Q), 0) // 8 == iota((160, Q), 1), 1.0, 0.0).astype(bf16)
    wide_in = jnp.dot(wint[...], rep, preferred_element_type=f32)
    wide_out = jnp.dot(wout[...], rep, preferred_element_type=f32)
    tall_out = jnp.dot(rept, wtout[...], preferred_element_type=f32)
    tall_in = jnp.dot(rept, wtin[...], preferred_element_type=f32)
    b = bias[...]
    high = b.astype(bf16).astype(f32)
    mid = (b - high).astype(bf16).astype(f32)
    low = b - high - mid
    col = iota((128, 160), 1)
    row = iota((160, 128), 0)
    biased = jnp.where(col == 152, high, jnp.where(col == 153, mid, jnp.where(col == 154, low, 0.0)))
    for k in range(8):
        own = (col % 8 == k) & (col < 152)
        own_row = (row % 8 == k) & (row < 152)
        part = slice(k * 128, k * 128 + 128)
        a_in[part, :] = jnp.where(own, wide_in, biased).astype(bf16)
        a_out[part, :] = jnp.where(own, wide_out, 0.0).astype(bf16)
        b_out[:, part] = jnp.where(own_row, tall_out, 0.0).astype(bf16)
        b_in[:, part] = jnp.where(own_row, tall_in, 0.0).astype(bf16)


def make_weights(weight_in, weight_out, bias_in):
    return pl.pallas_call(
        weights_kernel,
        out_shape=[jax.ShapeDtypeStruct((1024, 160), bf16)] * 2
        + [jax.ShapeDtypeStruct((160, 1024), bf16)] * 2,
        in_specs=vmem(5),
        out_specs=vmem(4),
        cost_estimate=pl.CostEstimate(flops=10**8, bytes_accessed=2 * 10**6, transcendentals=0),
    )(weight_in.T, weight_out, weight_in, weight_out.T, bias_in[:, None])


def pack_kernel(dist, cot, mask, up, down, cols, line):
    for out, rows in ((up, (126, 127)), (down, (0, 1))):
        for i, r in enumerate(rows):
            line[pl.ds(0, 38), :] = dist[pl.ds(r, 38, stride=128), :]
            line[pl.ds(38, 2), :] = mask[pl.ds(r, 2, stride=128), :].astype(f32)
            line[pl.ds(40, 38), :] = cot[pl.ds(r, 38, stride=128), :]
            line[pl.ds(78, 2), :] = jnp.zeros((2, 128), f32)
            out[pl.ds(i * 80, 80), :] = line[...].astype(bf16)
    lane, row = iota((8, 128), 1), iota((8, 128), 0)
    pick = jnp.zeros((8, 128), f32)
    for j, y in enumerate(COLS):
        pick = jnp.where((row == j) & (lane == y), 1.0, pick)
    pick = pick.astype(bf16)

    def slab(ref, i, place):
        values = ref[pl.ds(pl.multiple_of(i * 128, 128), 128), :].astype(f32).astype(bf16)
        got = lax.dot_general(pick, values, NT, preferred_element_type=f32)
        cols[pl.ds(place, 8, stride=IDX), :] = got

    def both(i, carry):
        slab(dist, i, i)
        slab(cot, i, i + 40)
        return carry

    lax.fori_loop(0, 38, both, 0)
    for z in range(2):
        slab(mask, z, 38 + z)
        cols[pl.ds(78 + z, 8, stride=IDX), :] = jnp.zeros((8, 128), f32)


def pack(dist, cot, mask):
    return pl.pallas_call(
        pack_kernel,
        out_shape=[jax.ShapeDtypeStruct((160, 128), bf16)] * 2 + [jax.ShapeDtypeStruct((640, 128), f32)],
        in_specs=vmem(3),
        out_specs=vmem(3),
        scratch_shapes=[pltpu.VMEM((80, 128), f32)],
    )(dist.reshape(38 * 128, 128), cot.reshape(38 * 128, 128), mask.reshape(256, 128))


def corner_kernel(from_up, from_down, cols, send_up, send_down, edge, lines):
    sides = ((from_down, 0, 0), (from_down, 1, 1), (from_up, 0, 126), (from_up, 1, 127))
    lane = iota((80, 128), 1)
    got = [ref[pl.ds(i * 80, 80), :].astype(f32) for ref, i, _ in sides]
    for (_, _, place), values in zip(sides, got):
        lines[pl.ds(place % 8, 80, stride=8), :] = values
    for r in range(2, 6):
        lines[pl.ds(r, 80, stride=8), :] = jnp.zeros((80, 128), f32)
    for j, y in enumerate(COLS):
        out = jnp.zeros((80, 128), f32)
        for (_, _, place), values in zip(sides, got):
            out = jnp.where(lane == place, values[:, y : y + 1], out)
        edge[pl.ds(j * 80, 80), :] = out
    for out, first in ((send_up, 0), (send_down, 6)):
        out[:, :128] = cols[pl.ds(first * 80, 160), :].astype(bf16)
        out[:, 128:] = edge[pl.ds(first * 80, 160), :].astype(bf16)


def corners(from_up, from_down, cols):
    return pl.pallas_call(
        corner_kernel,
        out_shape=[jax.ShapeDtypeStruct((160, 256), bf16)] * 2
        + [jax.ShapeDtypeStruct((640, 128), f32)] * 2,
        in_specs=vmem(3),
        out_specs=vmem(4),
    )(from_up, from_down, cols)


def main_kernel(
    dist, cot, mask, cols, edge, from_left, from_right, lines,
    a_in, a_out, b_out, b_in, bias_out,
    out, parts,
    post, gmid, gpad, hid, hpost, hcot, hmid, strip, spost, smid, flip, uo, acc, accb,
):
    lane = iota((8, 128), 1)
    row8 = iota((8, 128), 0)

    def pair(a, b):
        return jnp.concatenate([a, b], axis=1)

    strip[0] = cols[...]
    strip[1] = edge[...]
    strip[0, pl.ds(0, 160), :] = from_left[:, :128].astype(f32)
    strip[1, pl.ds(0, 160), :] = from_left[:, 128:].astype(f32)
    strip[0, pl.ds(480, 160), :] = from_right[:, :128].astype(f32)
    strip[1, pl.ds(480, 160), :] = from_right[:, 128:].astype(f32)

    def strip_of(i):
        return pair(strip[0, pl.ds(i, 8, stride=IDX), :], strip[1, pl.ds(i, 8, stride=IDX), :])

    def line_of(i):
        return lines[pl.ds(i * 8, 8), :]

    for q in range(Q):
        for z in range(2):
            i = 2 * q + z
            gpad[q, z, pl.ds(8, 128), :] = cot[q, z]
            halo = line_of(40 + i)
            gpad[q, z, pl.ds(0, 8), :] = halo
            gpad[q, z, pl.ds(136, 8), :] = halo
            gpad[q, z, pl.ds(144, 8), :] = cot[q, z, pl.ds(0, 8), :]

    uo[:, pl.ds(152, 8), :] = jnp.ones((2, 8, 128), f32)
    uo[:, pl.ds(312, 8), :] = jnp.ones((2, 8, 128), f32)
    acc[...] = jnp.zeros_like(acc)
    accb[...] = jnp.zeros_like(accb)
    flip[...] = jnp.zeros_like(flip)

    def stacked(values):
        both = jnp.concatenate(values, axis=0)
        return both

    def collide(d, solid, keep):
        ones = jnp.ones((8, 256), f32)
        field = stacked(d + [ones]).astype(bf16)
        t = jnp.tanh(jnp.dot(a_in[...], field, preferred_element_type=f32))
        if keep is not None:
            hid[keep] = t
        o = jnp.dot(b_out[...], t.astype(bf16), preferred_element_type=f32)
        res = []
        for q in range(Q):
            bias = bias_out[pl.ds(q * 8, 8), :]
            val = d[q] + o[q * 8 : q * 8 + 8] + pair(bias, bias)
            val = jnp.where(solid, d[OPP[q]], val)
            res.append(val.astype(bf16).astype(f32))
        return res

    def backward(u, g, solid, t, partial):
        og = [jnp.where(solid, 0.0, v) for v in g]
        ones = jnp.ones((8, 256), f32)
        if t is None:
            field = stacked(u + [ones]).astype(bf16)
            t = jnp.tanh(jnp.dot(a_in[...], field, preferred_element_type=f32))
        grad = stacked(og + [ones]).astype(bf16)
        hg = jnp.dot(a_out[...], grad, preferred_element_type=f32)
        hb = (hg * (1.0 - t * t)).astype(bf16)
        ig = jnp.dot(b_in[...], hb, preferred_element_type=f32)
        if partial:
            act = t.astype(bf16)
            for q in range(Q):
                for z in range(2):
                    uo[z, pl.ds(q * 8, 8), :] = u[q][:, z * 128 : z * 128 + 128]
                    uo[z, pl.ds(160 + q * 8, 8), :] = og[q][:, z * 128 : z * 128 + 128]
                accb[pl.ds(q * 8, 8), :] += og[q][:, :128] + og[q][:, 128:]
            total = acc[...]
            for k in range(8):
                left = pair(uo[0, pl.ds(k, 40, stride=8), :], uo[1, pl.ds(k, 40, stride=8), :])
                part = slice(k * 128, k * 128 + 128)
                right = jnp.concatenate([hb[part], act[part]], axis=0)
                total = total + lax.dot_general(left.astype(bf16), right, NT, preferred_element_type=f32)
            acc[...] = total
        return [
            og[q] + ig[q * 8 : q * 8 + 8] + jnp.where(solid, g[OPP[q]], 0.0) for q in range(Q)
        ]

    def streamed(ref, halo, row, orient):
        res = []
        for q in range(Q):
            cx, cy, cz = (orient * c for c in VEL[q])
            halves = []
            for z in range(2):
                zs = (z - cz) % 2
                v = ref[q, zs, pl.ds(row - cx, 8), :]
                if cy:
                    k = PLACE[q] * 2 + zs
                    h = halo[pl.ds(row - cx, 8), :][:, k : k + 1]
                    v = pltpu.roll(v, 1 if cy == 1 else 127, 1)
                    v = jnp.where(lane == (0 if cy == 1 else 127), h, v)
                halves.append(v)
            res.append(pair(*halves))
        return res

    def streamed_strip(get, orient, z):
        res = []
        for q in range(Q):
            cx, cy, cz = (orient * c for c in VEL[q])
            v = get(q, (z - cz) % 2)
            if cy:
                v = pltpu.roll(v, cy % 8, 0)
            if cx:
                v = pltpu.roll(v, cx % 256, 1)
            res.append(v)
        return res

    def to_halo(get, halo, orient):
        for q in SIDE:
            j = 1 if orient * VEL[q][1] == 1 else 6
            for z in range(2):
                flip[pl.ds(PLACE[q] * 2 + z, 1), :] = get(q, z, j)
        low = flip[:, :128].T
        high = flip[:, 128:].T
        halo[pl.ds(8, 128), :] = low
        outer = jnp.where(row8 < 4, high[0:8], high[120:128])
        halo[pl.ds(136, 8), :] = outer
        halo[pl.ds(0, 8), :] = outer
        halo[pl.ds(144, 8), :] = low[0:8]

    def put(ref, row, values):
        for q in range(Q):
            for z in range(2):
                ref[q, z, pl.ds(row, 8), :] = values[q][:, z * 128 : z * 128 + 128]

    def wrap(ref):
        for q in range(Q):
            for z in range(2):
                ref[q, z, pl.ds(0, 8), :] = ref[q, z, pl.ds(136, 8), :]
                ref[q, z, pl.ds(144, 8), :] = ref[q, z, pl.ds(8, 8), :]

    def block(ref, row):
        return [pair(ref[q, 0, pl.ds(row, 8), :], ref[q, 1, pl.ds(row, 8), :]) for q in range(Q)]

    def solid_at(row):
        return pair(mask[0, pl.ds(row, 8), :], mask[1, pl.ds(row, 8), :]) > 0

    line_solid = pair(line_of(38), line_of(39)) > 0.5

    def first(b, carry):
        row = pl.multiple_of(b * 8, 8)
        put(post, row + 8, collide(block(dist, row), solid_at(row), b))
        return carry

    lax.fori_loop(0, 16, first, 0)
    put(post, 136, collide([pair(line_of(2 * q), line_of(2 * q + 1)) for q in range(Q)], line_solid, None))
    wrap(post)
    for z in range(2):
        res = collide([strip_of(2 * q + z) for q in range(Q)], strip_of(38 + z) > 0.5, None)
        for q in range(Q):
            spost[z, q] = res[q]
    to_halo(lambda q, z, j: spost[z, q, pl.ds(j, 1), :], hpost, 1)
    to_halo(
        lambda q, z, j: pair(
            strip[0, pl.ds(j * IDX + 40 + 2 * q + z, 1), :], strip[1, pl.ds(j * IDX + 40 + 2 * q + z, 1), :]
        ),
        hcot,
        -1,
    )

    def second(b, carry):
        row = pl.multiple_of(b * 8, 8)
        u = streamed(post, hpost, row + 8, 1)
        g = streamed(gpad, hcot, row + 8, -1)
        put(gmid, row + 8, backward(u, g, solid_at(row), None, True))
        return carry

    lax.fori_loop(0, 16, second, 0)
    u = streamed(post, hpost, 136, 1)
    g = streamed(gpad, hcot, 136, -1)
    put(gmid, 136, backward(u, g, line_solid, None, False))
    wrap(gmid)
    for z in range(2):
        u = streamed_strip(lambda q, zs: spost[zs, q], 1, z)
        g = streamed_strip(lambda q, zs: strip_of(40 + 2 * q + zs), -1, z)
        res = backward(u, g, strip_of(38 + z) > 0.5, None, False)
        for q in range(Q):
            smid[z, q] = res[q]
    to_halo(lambda q, z, j: smid[z, q, pl.ds(j, 1), :], hmid, -1)

    def third(b, carry):
        row = pl.multiple_of(b * 8, 8)
        g = streamed(gmid, hmid, row + 8, -1)
        res = backward(block(dist, row), g, solid_at(row), hid[b], True)
        put(out, row, res)
        return carry

    lax.fori_loop(0, 16, third, 0)
    parts[pl.ds(0, 20), :] = acc[pl.ds(0, 20), pl.ds(0, 128)]
    parts[pl.ds(20, 20), :] = acc[pl.ds(20, 20), pl.ds(128, 128)]
    for q in range(Q):
        parts[pl.ds(40 + q, 1), :] = jnp.sum(accb[pl.ds(q * 8, 8), :], axis=0, keepdims=True)
    parts[pl.ds(59, 5), :] = jnp.zeros((5, 128), f32)


def main_call(*args):
    field = pltpu.VMEM((Q, 2, 152, 128), f32)
    halo = pltpu.VMEM((152, 128), f32)
    return pl.pallas_call(
        main_kernel,
        out_shape=[jax.ShapeDtypeStruct((Q, 2, 128, 128), f32), jax.ShapeDtypeStruct((64, 128), f32)],
        in_specs=vmem(len(args)),
        out_specs=vmem(2),
        scratch_shapes=[
            field, field, field,
            pltpu.VMEM((16, 1024, 256), f32),
            halo, halo, halo,
            pltpu.VMEM((2, 640, 128), f32),
            pltpu.VMEM((2, Q, 8, 256), f32),
            pltpu.VMEM((2, Q, 8, 256), f32),
            pltpu.VMEM((128, 256), f32),
            pltpu.VMEM((2, 320, 128), f32),
            pltpu.VMEM((40, 256), f32),
            pltpu.VMEM((152, 128), f32),
        ],
        compiler_params=pltpu.CompilerParams(vmem_limit_bytes=58 * 2**20),
    )(*args)


def neighbours(axis):
    size = lax.axis_size(axis)
    up = [(i, (i + 1) % size) for i in range(size)]
    return up, [(j, i) for i, j in up]


def summed(values):
    for axis in ("gx", "gy"):
        size = lax.axis_size(axis)
        step = 1
        while step < size:
            values = values + lax.ppermute(values, axis, [(i, i ^ step) for i in range(size)])
            step *= 2
    return values


def shards(dist, cot, mask, weight_in, bias_in, weight_out, bias_out):
    send_up, send_down, cols = pack(dist, cot, mask)
    up, down = neighbours("gx")
    from_up = lax.ppermute(send_up, "gx", up)
    from_down = lax.ppermute(send_down, "gx", down)
    nets = make_weights(weight_in, weight_out, bias_in)
    side_up, side_down, edge, lines = corners(from_up, from_down, cols)
    up, down = neighbours("gy")
    from_left = lax.ppermute(side_up, "gy", up)
    from_right = lax.ppermute(side_down, "gy", down)
    bias_rows = jnp.broadcast_to(jnp.repeat(bias_out, 8)[:, None], (152, 128))
    grad, parts = main_call(dist, cot, mask, cols, edge, from_left, from_right, lines, *nets, bias_rows)
    total = summed(parts)
    cells = mask.size * lax.axis_size("gx") * lax.axis_size("gy")
    total = total * (1.0 / math.sqrt(cells))
    return grad, total[:19], total[19], total[20:39].T, jnp.sum(total[40:59], axis=1)


def solution(mesh):
    field = P(None, None, "gx", "gy")
    return jax.shard_map(
        shards,
        mesh=mesh,
        in_specs=(field, field, P(None, "gx", "gy"), P(), P(), P(), P()),
        out_specs=(field, P(), P(), P(), P()),
        check_vma=False,
    )
```

```python
import math

import jax
import jax.numpy as jnp
from jax import lax
from jax.experimental import pallas as pl
from jax.experimental.pallas import tpu as pltpu
from jax.sharding import PartitionSpec as P

VEL = (
    (0, 0, 0), (1, 0, 0), (-1, 0, 0), (0, 1, 0), (0, -1, 0), (0, 0, 1), (0, 0, -1),
    (1, 1, 0), (-1, -1, 0), (1, -1, 0), (-1, 1, 0), (1, 0, 1), (-1, 0, -1), (1, 0, -1),
    (-1, 0, 1), (0, 1, 1), (0, -1, -1), (0, 1, -1), (0, -1, 1),
)
OPP = (0, 2, 1, 4, 3, 6, 5, 8, 7, 10, 9, 12, 11, 14, 13, 16, 15, 18, 17)
Q = 19
WIDE = 2
STEPS = 16 // WIDE
SIDE = tuple(q for q in range(Q) if VEL[q][1])
PLACE = {q: i for i, q in enumerate(SIDE)}
f32 = jnp.float32
bf16 = jnp.bfloat16
NT = (((1,), (1,)), ((), ()))
IDX = 80
COLS = (126, 127, 0, 0, 127, 127, 0, 1)


def iota(shape, dim):
    return lax.broadcasted_iota(jnp.int32, shape, dim)


def vmem(n):
    return [pl.BlockSpec(memory_space=pltpu.VMEM)] * n


def weights_kernel(win, wout, bias, bias_out, a_in, a_out, b_out, b_in, bias_rows):
    TN = (((0,), (0,)), ((), ()))
    rep = jnp.where(iota((Q, 160), 1) // 8 == iota((Q, 160), 0), 1.0, 0.0).astype(bf16)
    rept = jnp.where(iota((160, Q), 0) // 8 == iota((160, Q), 1), 1.0, 0.0).astype(bf16)
    wide_in = lax.dot_general(win[...], rep, TN, preferred_element_type=f32)
    wide_out = jnp.dot(wout[...], rep, preferred_element_type=f32)
    tall_out = lax.dot_general(rept, wout[...], NT, preferred_element_type=f32)
    tall_in = jnp.dot(rept, win[...], preferred_element_type=f32)
    b = jnp.broadcast_to(bias[...], (128, 128)).T
    b = jnp.concatenate([b, b[:, :32]], axis=1)
    high = b.astype(bf16).astype(f32)
    mid = (b - high).astype(bf16).astype(f32)
    low = b - high - mid
    col = iota((128, 160), 1)
    row = iota((160, 128), 0)
    biased = jnp.where(col == 152, high, jnp.where(col == 153, mid, jnp.where(col == 154, low, 0.0)))
    for k in range(8):
        own = (col % 8 == k) & (col < 152)
        own_row = (row % 8 == k) & (row < 152)
        part = slice(k * 128, k * 128 + 128)
        a_in[part, :] = jnp.where(own, wide_in, biased).astype(bf16)
        a_out[part, :] = jnp.where(own, wide_out, 0.0).astype(bf16)
        b_out[:, part] = jnp.where(own_row, tall_out, 0.0).astype(bf16)
        b_in[:, part] = jnp.where(own_row, tall_in, 0.0).astype(bf16)
    for q in range(Q):
        bias_rows[pl.ds(q * 8, 8), :] = jnp.broadcast_to(bias_out[0:1, q : q + 1], (8, 128))


def make_weights(weight_in, weight_out, bias_in, bias_out):
    return pl.pallas_call(
        weights_kernel,
        out_shape=[jax.ShapeDtypeStruct((1024, 160), bf16)] * 2
        + [jax.ShapeDtypeStruct((160, 1024), bf16)] * 2
        + [jax.ShapeDtypeStruct((152, 128), f32)],
        in_specs=vmem(4),
        out_specs=vmem(5),
        cost_estimate=pl.CostEstimate(flops=10**8, bytes_accessed=2 * 10**6, transcendentals=0),
    )(weight_in, weight_out, bias_in[None], bias_out[None])


def pack_kernel(dist, cot, mask, up, down, cols, line):
    for out, rows in ((up, (126, 127)), (down, (0, 1))):
        for i, r in enumerate(rows):
            line[pl.ds(0, 38), :] = dist[pl.ds(r, 38, stride=128), :]
            line[pl.ds(38, 2), :] = mask[pl.ds(r, 2, stride=128), :].astype(f32)
            line[pl.ds(40, 38), :] = cot[pl.ds(r, 38, stride=128), :]
            line[pl.ds(78, 2), :] = jnp.zeros((2, 128), f32)
            out[pl.ds(i * 80, 80), :] = line[...].astype(bf16)
    lane, row = iota((8, 128), 1), iota((8, 128), 0)
    pick = jnp.zeros((8, 128), f32)
    for j, y in enumerate(COLS):
        pick = jnp.where((row == j) & (lane == y), 1.0, pick)
    pick = pick.astype(bf16)

    def slabs(ref, first, count, place):
        values = ref[pl.ds(first * 128, count * 128), :].astype(f32).astype(bf16)
        got = lax.dot_general(pick, values, NT, preferred_element_type=f32)
        for i in range(count):
            cols[pl.ds(place + i, 8, stride=IDX), :] = got[:, i * 128 : i * 128 + 128]

    for half in range(2):
        slabs(dist, half * 19, 19, half * 19)
        slabs(cot, half * 19, 19, 40 + half * 19)
    slabs(mask, 0, 2, 38)
    for z in range(2):
        cols[pl.ds(78 + z, 8, stride=IDX), :] = jnp.zeros((8, 128), f32)


def pack(dist, cot, mask):
    return pl.pallas_call(
        pack_kernel,
        out_shape=[jax.ShapeDtypeStruct((160, 128), bf16)] * 2 + [jax.ShapeDtypeStruct((640, 128), f32)],
        in_specs=vmem(3),
        out_specs=vmem(3),
        scratch_shapes=[pltpu.VMEM((80, 128), f32)],
    )(dist.reshape(38 * 128, 128), cot.reshape(38 * 128, 128), mask.reshape(256, 128))


def corner_kernel(from_up, from_down, cols, send_up, send_down, edge, lines):
    sides = ((from_down, 0, 0), (from_down, 1, 1), (from_up, 0, 126), (from_up, 1, 127))
    lane = iota((80, 128), 1)
    got = [ref[pl.ds(i * 80, 80), :].astype(f32) for ref, i, _ in sides]
    for (_, _, place), values in zip(sides, got):
        lines[pl.ds(place % 8, 80, stride=8), :] = values
    for r in range(2, 6):
        lines[pl.ds(r, 80, stride=8), :] = jnp.zeros((80, 128), f32)
    for j, y in enumerate(COLS):
        out = jnp.zeros((80, 128), f32)
        for (_, _, place), values in zip(sides, got):
            out = jnp.where(lane == place, values[:, y : y + 1], out)
        edge[pl.ds(j * 80, 80), :] = out
    for out, first in ((send_up, 0), (send_down, 6)):
        out[:, :128] = cols[pl.ds(first * 80, 160), :].astype(bf16)
        out[:, 128:] = edge[pl.ds(first * 80, 160), :].astype(bf16)


def corners(from_up, from_down, cols):
    return pl.pallas_call(
        corner_kernel,
        out_shape=[jax.ShapeDtypeStruct((160, 256), bf16)] * 2
        + [jax.ShapeDtypeStruct((640, 128), f32)] * 2,
        in_specs=vmem(3),
        out_specs=vmem(4),
    )(from_up, from_down, cols)


def main_kernel(
    dist, cot, mask, cols, edge, from_left, from_right, lines,
    a_in, a_out, b_out, b_in, bias_out,
    out, parts,
    post, gmid, gpad, hid, hpost, hcot, hmid, strip, spost, smid, flip, uo, acc_in, acc_out, accb,
):
    lane = iota((8, 128), 1)
    row8 = iota((8, 128), 0)

    def join(*parts):
        return jnp.concatenate(parts, axis=1)

    strip[0] = cols[...]
    strip[1] = edge[...]
    strip[0, pl.ds(0, 160), :] = from_left[:, :128].astype(f32)
    strip[1, pl.ds(0, 160), :] = from_left[:, 128:].astype(f32)
    strip[0, pl.ds(480, 160), :] = from_right[:, :128].astype(f32)
    strip[1, pl.ds(480, 160), :] = from_right[:, 128:].astype(f32)

    def strip_of(i):
        return join(strip[0, pl.ds(i, 8, stride=IDX), :], strip[1, pl.ds(i, 8, stride=IDX), :])

    def line_of(i):
        return lines[pl.ds(i * 8, 8), :]

    for q in range(Q):
        for z in range(2):
            i = 2 * q + z
            gpad[q, z, pl.ds(8, 128), :] = cot[q, z]
            halo = line_of(40 + i)
            gpad[q, z, pl.ds(0, 8), :] = halo
            gpad[q, z, pl.ds(136, 8), :] = halo
            gpad[q, z, pl.ds(144, 8), :] = cot[q, z, pl.ds(0, 8), :]

    uo[:, pl.ds(152, 8), :] = jnp.ones((2 * WIDE, 8, 128), f32)
    uo[:, pl.ds(312, 8), :] = jnp.ones((2 * WIDE, 8, 128), f32)
    acc_in[...] = jnp.zeros_like(acc_in)
    acc_out[...] = jnp.zeros_like(acc_out)
    accb[...] = jnp.zeros_like(accb)
    flip[...] = jnp.zeros_like(flip)

    def operand(values):
        ones = jnp.ones(values[0].shape, f32)
        return jnp.concatenate(values + [ones], axis=0).astype(bf16)

    def hidden(values):
        return jnp.tanh(jnp.dot(a_in[...], operand(values), preferred_element_type=f32))

    def collide(d, solid, keep):
        t = hidden(d)
        if keep is not None:
            hid[keep] = t
        o = jnp.dot(b_out[...], t.astype(bf16), preferred_element_type=f32)
        res = []
        for q in range(Q):
            bias = bias_out[pl.ds(q * 8, 8), :]
            val = d[q] + o[q * 8 : q * 8 + 8] + join(*[bias] * (d[q].shape[1] // 128))
            val = jnp.where(solid, d[OPP[q]], val)
            res.append(val.astype(bf16).astype(f32))
        return res

    def backward(u, g, solid, t, partial):
        og = [jnp.where(solid, 0.0, v) for v in g]
        if t is None:
            t = hidden(u)
        hg = jnp.dot(a_out[...], operand(og), preferred_element_type=f32)
        hb = (hg * (1.0 - t * t)).astype(bf16)
        ig = jnp.dot(b_in[...], hb, preferred_element_type=f32)
        if partial:
            act = t.astype(bf16)
            halves = [slice(h * 128, h * 128 + 128) for h in range(2 * WIDE)]
            for q in range(Q):
                for h, part in enumerate(halves):
                    uo[h, pl.ds(q * 8, 8), :] = u[q][:, part]
                    uo[h, pl.ds(160 + q * 8, 8), :] = og[q][:, part]
                accb[pl.ds(q * 8, 8), :] += sum(og[q][:, part] for part in halves)

            def cells(first):
                return join(
                    *[uo[h, pl.ds(first + k, 20, stride=8), :] for k in range(8) for h in range(2 * WIDE)]
                ).astype(bf16)

            def units(values):
                return join(*[values[k * 128 : k * 128 + 128] for k in range(8)])

            acc_in[:, :20] += lax.dot_general(units(hb), cells(0), NT, preferred_element_type=f32)
            acc_out[...] += lax.dot_general(cells(160), units(act), NT, preferred_element_type=f32)
        return [
            og[q] + ig[q * 8 : q * 8 + 8] + jnp.where(solid, g[OPP[q]], 0.0) for q in range(Q)
        ]

    def streamed(ref, halo, rows, orient):
        res = []
        for q in range(Q):
            cx, cy, cz = (orient * c for c in VEL[q])
            pieces = []
            for row in rows:
                for z in range(2):
                    zs = (z - cz) % 2
                    v = ref[q, zs, pl.ds(row - cx, 8), :]
                    if cy:
                        k = PLACE[q] * 2 + zs
                        h = halo[pl.ds(row - cx, 8), :][:, k : k + 1]
                        v = pltpu.roll(v, 1 if cy == 1 else 127, 1)
                        v = jnp.where(lane == (0 if cy == 1 else 127), h, v)
                    pieces.append(v)
            res.append(join(*pieces))
        return res

    def streamed_strip(get, orient, z):
        res = []
        for q in range(Q):
            cx, cy, cz = (orient * c for c in VEL[q])
            v = get(q, (z - cz) % 2)
            if cy:
                v = pltpu.roll(v, cy % 8, 0)
            if cx:
                v = pltpu.roll(v, cx % 256, 1)
            res.append(v)
        return res

    def to_halo(get, halo, orient):
        for q in SIDE:
            j = 1 if orient * VEL[q][1] == 1 else 6
            for z in range(2):
                flip[pl.ds(PLACE[q] * 2 + z, 1), :] = get(q, z, j)
        low = flip[:, :128].T
        high = flip[:, 128:].T
        halo[pl.ds(8, 128), :] = low
        outer = jnp.where(row8 < 4, high[0:8], high[120:128])
        halo[pl.ds(136, 8), :] = outer
        halo[pl.ds(0, 8), :] = outer
        halo[pl.ds(144, 8), :] = low[0:8]

    def put(ref, rows, values):
        for q in range(Q):
            for i, row in enumerate(rows):
                for z in range(2):
                    at = i * 256 + z * 128
                    ref[q, z, pl.ds(row, 8), :] = values[q][:, at : at + 128]

    def put_outer(ref, side, values):
        for q in range(Q):
            for z in range(2):
                ref[q, z, pl.ds(136, 8), :] = values[q][:, z * 128 : z * 128 + 128]
                ref[q, z, pl.ds(0, 8), :] = values[q][:, z * 128 : z * 128 + 128]
                ref[q, z, pl.ds(144, 8), :] = ref[q, z, pl.ds(8, 8), :]
                side[z, q] = values[q][:, 256 + z * 256 : 512 + z * 256]

    def block(ref, rows):
        return [join(*[ref[q, z, pl.ds(r, 8), :] for r in rows for z in range(2)]) for q in range(Q)]

    def solid_at(rows):
        return join(*[mask[z, pl.ds(r, 8), :] for r in rows for z in range(2)]) > 0

    outer_solid = join(line_of(38), line_of(39), strip_of(38), strip_of(39)) > 0.5

    def rows_of(b, offset):
        return [pl.multiple_of((b + w * STEPS) * 8, 8) + offset for w in range(WIDE)]

    def first(b, carry):
        put(post, rows_of(b, 8), collide(block(dist, rows_of(b, 0)), solid_at(rows_of(b, 0)), b))
        return carry

    lax.fori_loop(0, STEPS, first, 0)
    d = [
        join(line_of(2 * q), line_of(2 * q + 1), strip_of(2 * q), strip_of(2 * q + 1)) for q in range(Q)
    ]
    put_outer(post, spost, collide(d, outer_solid, None))
    to_halo(lambda q, z, j: spost[z, q, pl.ds(j, 1), :], hpost, 1)
    to_halo(
        lambda q, z, j: join(
            strip[0, pl.ds(j * IDX + 40 + 2 * q + z, 1), :], strip[1, pl.ds(j * IDX + 40 + 2 * q + z, 1), :]
        ),
        hcot,
        -1,
    )

    def second(b, carry):
        u = streamed(post, hpost, rows_of(b, 8), 1)
        g = streamed(gpad, hcot, rows_of(b, 8), -1)
        put(gmid, rows_of(b, 8), backward(u, g, solid_at(rows_of(b, 0)), None, True))
        return carry

    lax.fori_loop(0, STEPS, second, 0)
    us = [streamed(post, hpost, [136], 1)] + [
        streamed_strip(lambda q, zs: spost[zs, q], 1, z) for z in range(2)
    ]
    gs = [streamed(gpad, hcot, [136], -1)] + [
        streamed_strip(lambda q, zs: strip_of(40 + 2 * q + zs), -1, z) for z in range(2)
    ]
    u = [join(*[v[q] for v in us]) for q in range(Q)]
    g = [join(*[v[q] for v in gs]) for q in range(Q)]
    put_outer(gmid, smid, backward(u, g, outer_solid, None, False))
    to_halo(lambda q, z, j: smid[z, q, pl.ds(j, 1), :], hmid, -1)

    def third(b, carry):
        g = streamed(gmid, hmid, rows_of(b, 8), -1)
        rows = rows_of(b, 0)
        put(out, rows, backward(block(dist, rows), g, solid_at(rows), hid[b], True))
        return carry

    lax.fori_loop(0, STEPS, third, 0)
    parts[pl.ds(0, 20), :] = acc_in[...].T[:20]
    parts[pl.ds(20, 20), :] = acc_out[...]
    for q in range(Q):
        parts[pl.ds(40 + q, 1), :] = jnp.sum(accb[pl.ds(q * 8, 8), :], axis=0, keepdims=True)
    parts[pl.ds(59, 5), :] = jnp.zeros((5, 128), f32)


def main_call(*args):
    field = pltpu.VMEM((Q, 2, 152, 128), f32)
    halo = pltpu.VMEM((152, 128), f32)
    return pl.pallas_call(
        main_kernel,
        out_shape=[jax.ShapeDtypeStruct((Q, 2, 128, 128), f32), jax.ShapeDtypeStruct((64, 128), f32)],
        in_specs=vmem(len(args)),
        out_specs=vmem(2),
        scratch_shapes=[
            field, field, field,
            pltpu.VMEM((STEPS, 1024, 256 * WIDE), f32),
            halo, halo, halo,
            pltpu.VMEM((2, 640, 128), f32),
            pltpu.VMEM((2, Q, 8, 256), f32),
            pltpu.VMEM((2, Q, 8, 256), f32),
            pltpu.VMEM((128, 256), f32),
            pltpu.VMEM((2 * WIDE, 320, 128), f32),
            pltpu.VMEM((128, 128), f32),
            pltpu.VMEM((20, 128), f32),
            pltpu.VMEM((152, 128), f32),
        ],
        compiler_params=pltpu.CompilerParams(vmem_limit_bytes=58 * 2**20),
    )(*args)


def neighbours(axis):
    size = lax.axis_size(axis)
    up = [(i, (i + 1) % size) for i in range(size)]
    return up, [(j, i) for i, j in up]


def summed(values):
    shape = {axis: lax.axis_size(axis) for axis in ("gx", "gy")}
    nx, ny = shape["gx"], shape["gy"]

    def flat(partner):
        pairs = []
        for x in range(nx):
            for y in range(ny):
                px, py = partner(x, y)
                pairs.append((x * ny + y, px * ny + py))
        return pairs

    stages = []
    if (nx, ny) == (8, 16):
        other = (3, 2, 1, 0)
        stages = [
            lambda x, y: (x, y ^ 1),
            lambda x, y: (x ^ 1, y),
            lambda x, y: (x ^ 1, y ^ 2),
            lambda x, y: (x ^ 2, y),
            lambda x, y: (other[x // 2] * 2 + x % 2, y),
            lambda x, y: (x, y ^ 4),
            lambda x, y: (x, other[y // 4] * 4 + y % 4),
        ]
    else:
        for k in range(nx.bit_length() - 1):
            stages.append(lambda x, y, k=k: (x ^ (1 << k), y))
        for k in range(ny.bit_length() - 1):
            stages.append(lambda x, y, k=k: (x, y ^ (1 << k)))
    for partner in stages:
        values = values + lax.ppermute(values, ("gx", "gy"), flat(partner))
    return values


def shards(dist, cot, mask, weight_in, bias_in, weight_out, bias_out):
    send_up, send_down, cols = pack(dist, cot, mask)
    up, down = neighbours("gx")
    from_up = lax.ppermute(send_up, "gx", up)
    from_down = lax.ppermute(send_down, "gx", down)
    nets = make_weights(weight_in, weight_out, bias_in, bias_out)
    side_up, side_down, edge, lines = corners(from_up, from_down, cols)
    up, down = neighbours("gy")
    from_left = lax.ppermute(side_up, "gy", up)
    from_right = lax.ppermute(side_down, "gy", down)
    grad, parts = main_call(dist, cot, mask, cols, edge, from_left, from_right, lines, *nets)
    total = summed(parts)
    cells = mask.size * lax.axis_size("gx") * lax.axis_size("gy")
    total = total * (1.0 / math.sqrt(cells))
    return grad, total[:19], total[19], total[20:39].T, jnp.sum(total[40:59], axis=1)


def solution(mesh):
    field = P(None, None, "gx", "gy")
    return jax.shard_map(
        shards,
        mesh=mesh,
        in_specs=(field, field, P(None, "gx", "gy"), P(), P(), P(), P()),
        out_specs=(field, P(), P(), P(), P()),
        check_vma=False,
    )
```

```python
import math

import jax
import jax.numpy as jnp
from jax import lax
from jax.experimental import pallas as pl
from jax.experimental.pallas import tpu as pltpu
from jax.sharding import PartitionSpec as P

VEL = (
    (0, 0, 0), (1, 0, 0), (-1, 0, 0), (0, 1, 0), (0, -1, 0), (0, 0, 1), (0, 0, -1),
    (1, 1, 0), (-1, -1, 0), (1, -1, 0), (-1, 1, 0), (1, 0, 1), (-1, 0, -1), (1, 0, -1),
    (-1, 0, 1), (0, 1, 1), (0, -1, -1), (0, 1, -1), (0, -1, 1),
)
OPP = (0, 2, 1, 4, 3, 6, 5, 8, 7, 10, 9, 12, 11, 14, 13, 16, 15, 18, 17)
Q = 19
WIDE = 4
STEPS = 16 // WIDE
SIDE = tuple(q for q in range(Q) if VEL[q][1])
PLACE = {q: i for i, q in enumerate(SIDE)}
f32 = jnp.float32
bf16 = jnp.bfloat16
NT = (((1,), (1,)), ((), ()))
IDX = 80
COLS = (126, 127, 0, 0, 127, 127, 0, 1)


def iota(shape, dim):
    return lax.broadcasted_iota(jnp.int32, shape, dim)


def vmem(n):
    return [pl.BlockSpec(memory_space=pltpu.VMEM)] * n


def weights_kernel(win, wout, bias, bias_out, a_in, a_out, b_out, b_in, bias_rows):
    TN = (((0,), (0,)), ((), ()))
    rep = jnp.where(iota((Q, 160), 1) // 8 == iota((Q, 160), 0), 1.0, 0.0).astype(bf16)
    rept = jnp.where(iota((160, Q), 0) // 8 == iota((160, Q), 1), 1.0, 0.0).astype(bf16)
    wide_in = lax.dot_general(win[...], rep, TN, preferred_element_type=f32)
    wide_out = jnp.dot(wout[...], rep, preferred_element_type=f32)
    tall_out = lax.dot_general(rept, wout[...], NT, preferred_element_type=f32)
    tall_in = jnp.dot(rept, win[...], preferred_element_type=f32)
    b = jnp.broadcast_to(bias[...], (128, 128)).T
    b = jnp.concatenate([b, b[:, :32]], axis=1)
    high = b.astype(bf16).astype(f32)
    mid = (b - high).astype(bf16).astype(f32)
    low = b - high - mid
    col = iota((128, 160), 1)
    row = iota((160, 128), 0)
    biased = jnp.where(col == 152, high, jnp.where(col == 153, mid, jnp.where(col == 154, low, 0.0)))
    for k in range(8):
        own = (col % 8 == k) & (col < 152)
        own_row = (row % 8 == k) & (row < 152)
        part = slice(k * 128, k * 128 + 128)
        a_in[part, :] = jnp.where(own, wide_in, biased).astype(bf16)
        a_out[part, :] = jnp.where(own, wide_out, 0.0).astype(bf16)
        b_out[:, part] = jnp.where(own_row, tall_out, 0.0).astype(bf16)
        b_in[:, part] = jnp.where(own_row, tall_in, 0.0).astype(bf16)
    for q in range(Q):
        bias_rows[pl.ds(q * 8, 8), :] = jnp.broadcast_to(bias_out[0:1, q : q + 1], (8, 128))


def make_weights(weight_in, weight_out, bias_in, bias_out):
    return pl.pallas_call(
        weights_kernel,
        out_shape=[jax.ShapeDtypeStruct((1024, 160), bf16)] * 2
        + [jax.ShapeDtypeStruct((160, 1024), bf16)] * 2
        + [jax.ShapeDtypeStruct((152, 128), f32)],
        in_specs=vmem(4),
        out_specs=vmem(5),
        cost_estimate=pl.CostEstimate(flops=10**8, bytes_accessed=2 * 10**6, transcendentals=0),
    )(weight_in, weight_out, bias_in[None], bias_out[None])


def pack_kernel(dist, cot, mask, up, down, cols, line):
    for out, rows in ((up, (126, 127)), (down, (0, 1))):
        for i, r in enumerate(rows):
            line[pl.ds(0, 38), :] = dist[pl.ds(r, 38, stride=128), :]
            line[pl.ds(38, 2), :] = mask[pl.ds(r, 2, stride=128), :].astype(f32)
            line[pl.ds(40, 38), :] = cot[pl.ds(r, 38, stride=128), :]
            line[pl.ds(78, 2), :] = jnp.zeros((2, 128), f32)
            out[pl.ds(i * 80, 80), :] = line[...].astype(bf16)
    lane, row = iota((8, 128), 1), iota((8, 128), 0)
    pick = jnp.zeros((8, 128), f32)
    for j, y in enumerate(COLS):
        pick = jnp.where((row == j) & (lane == y), 1.0, pick)
    pick = pick.astype(bf16)

    def slabs(ref, first, count, place):
        values = ref[pl.ds(first * 128, count * 128), :].astype(f32).astype(bf16)
        got = lax.dot_general(pick, values, NT, preferred_element_type=f32)
        for i in range(count):
            cols[pl.ds(place + i, 8, stride=IDX), :] = got[:, i * 128 : i * 128 + 128]

    for half in range(2):
        slabs(dist, half * 19, 19, half * 19)
        slabs(cot, half * 19, 19, 40 + half * 19)
    slabs(mask, 0, 2, 38)
    for z in range(2):
        cols[pl.ds(78 + z, 8, stride=IDX), :] = jnp.zeros((8, 128), f32)


def pack(dist, cot, mask):
    return pl.pallas_call(
        pack_kernel,
        out_shape=[jax.ShapeDtypeStruct((160, 128), bf16)] * 2 + [jax.ShapeDtypeStruct((640, 128), f32)],
        in_specs=vmem(3),
        out_specs=vmem(3),
        scratch_shapes=[pltpu.VMEM((80, 128), f32)],
    )(dist.reshape(38 * 128, 128), cot.reshape(38 * 128, 128), mask.reshape(256, 128))


def corner_kernel(from_up, from_down, cols, send_up, send_down, edge, lines):
    sides = ((from_down, 0, 0), (from_down, 1, 1), (from_up, 0, 126), (from_up, 1, 127))
    lane = iota((80, 128), 1)
    got = [ref[pl.ds(i * 80, 80), :].astype(f32) for ref, i, _ in sides]
    for (_, _, place), values in zip(sides, got):
        lines[pl.ds(place % 8, 80, stride=8), :] = values
    for r in range(2, 6):
        lines[pl.ds(r, 80, stride=8), :] = jnp.zeros((80, 128), f32)
    for j, y in enumerate(COLS):
        out = jnp.zeros((80, 128), f32)
        for (_, _, place), values in zip(sides, got):
            out = jnp.where(lane == place, values[:, y : y + 1], out)
        edge[pl.ds(j * 80, 80), :] = out
    for out, first in ((send_up, 0), (send_down, 6)):
        out[:, :128] = cols[pl.ds(first * 80, 160), :].astype(bf16)
        out[:, 128:] = edge[pl.ds(first * 80, 160), :].astype(bf16)


def corners(from_up, from_down, cols):
    return pl.pallas_call(
        corner_kernel,
        out_shape=[jax.ShapeDtypeStruct((160, 256), bf16)] * 2
        + [jax.ShapeDtypeStruct((640, 128), f32)] * 2,
        in_specs=vmem(3),
        out_specs=vmem(4),
    )(from_up, from_down, cols)


def main_kernel(
    dist, cot, mask, cols, edge, from_left, from_right, lines,
    a_in, a_out, b_out, b_in, bias_out,
    out, parts,
    post, gmid, gpad, hid, hpost, hcot, hmid, strip, spost, smid, flip, uo, acc_in, acc_out, accb,
):
    lane = iota((8, 128), 1)
    row8 = iota((8, 128), 0)

    def join(*parts):
        return jnp.concatenate(parts, axis=1)

    strip[0] = cols[...]
    strip[1] = edge[...]
    strip[0, pl.ds(0, 160), :] = from_left[:, :128].astype(f32)
    strip[1, pl.ds(0, 160), :] = from_left[:, 128:].astype(f32)
    strip[0, pl.ds(480, 160), :] = from_right[:, :128].astype(f32)
    strip[1, pl.ds(480, 160), :] = from_right[:, 128:].astype(f32)

    def strip_of(i):
        return join(strip[0, pl.ds(i, 8, stride=IDX), :], strip[1, pl.ds(i, 8, stride=IDX), :])

    def line_of(i):
        return lines[pl.ds(i * 8, 8), :]

    for q in range(Q):
        for z in range(2):
            i = 2 * q + z
            gpad[q, z, pl.ds(8, 128), :] = cot[q, z]
            halo = line_of(40 + i)
            gpad[q, z, pl.ds(0, 8), :] = halo
            gpad[q, z, pl.ds(136, 8), :] = halo
            gpad[q, z, pl.ds(144, 8), :] = cot[q, z, pl.ds(0, 8), :]

    uo[...] = jnp.zeros_like(uo)
    uo[:, pl.ds(19 * 9, 9), :] = jnp.ones((2 * WIDE, 9, 128), f32)
    acc_in[...] = jnp.zeros_like(acc_in)
    acc_out[...] = jnp.zeros_like(acc_out)
    accb[...] = jnp.zeros_like(accb)
    flip[...] = jnp.zeros_like(flip)

    def operand(values):
        ones = jnp.ones(values[0].shape, f32)
        return jnp.concatenate(values + [ones], axis=0).astype(bf16)

    def hidden(values):
        return jnp.tanh(jnp.dot(a_in[...], operand(values), preferred_element_type=f32))

    def collide(d, solid, keep):
        t = hidden(d)
        if keep is not None:
            hid[keep] = t
        o = jnp.dot(b_out[...], t.astype(bf16), preferred_element_type=f32)
        res = []
        for q in range(Q):
            bias = bias_out[pl.ds(q * 8, 8), :]
            val = d[q] + o[q * 8 : q * 8 + 8] + join(*[bias] * (d[q].shape[1] // 128))
            val = jnp.where(solid, d[OPP[q]], val)
            res.append(val.astype(bf16).astype(f32))
        return res

    def backward(u, g, solid, t, partial):
        og = [jnp.where(solid, 0.0, v) for v in g]
        if t is None:
            t = hidden(u)
        hg = jnp.dot(a_out[...], operand(og), preferred_element_type=f32)
        hb = (hg * (1.0 - t * t)).astype(bf16)
        ig = jnp.dot(b_in[...], hb, preferred_element_type=f32)
        if partial:
            act = t.astype(bf16)
            halves = [slice(h * 128, h * 128 + 128) for h in range(2 * WIDE)]
            for q in range(Q):
                for h, part in enumerate(halves):
                    uo[h, pl.ds(q * 9, 8), :] = u[q][:, part]
                    uo[h, pl.ds(216 + q * 9, 8), :] = og[q][:, part]
                accb[pl.ds(q * 8, 8), :] += sum(og[q][:, part] for part in halves)

            def cells(first):
                lines24 = join(
                    *[uo[h, pl.ds(first + k, 24, stride=9), :] for k in range(8) for h in range(2 * WIDE)]
                )
                return jnp.concatenate([lines24, jnp.zeros((8, lines24.shape[1]), f32)], axis=0).astype(bf16)

            def units(values):
                return join(*[values[k * 128 : k * 128 + 128] for k in range(8)])

            left = jnp.concatenate([units(hb), cells(216)], axis=0)
            right = jnp.concatenate([units(act), cells(0)], axis=0)
            both = lax.dot_general(left, right, NT, preferred_element_type=f32)
            acc_in[:, :32] += both[:128, 128:]
            acc_out[...] += both[128:, :128]
        return [
            og[q] + ig[q * 8 : q * 8 + 8] + jnp.where(solid, g[OPP[q]], 0.0) for q in range(Q)
        ]

    def streamed(ref, halo, rows, orient):
        res = []
        for q in range(Q):
            cx, cy, cz = (orient * c for c in VEL[q])
            pieces = []
            for row in rows:
                for z in range(2):
                    zs = (z - cz) % 2
                    v = ref[q, zs, pl.ds(row - cx, 8), :]
                    if cy:
                        k = PLACE[q] * 2 + zs
                        h = halo[pl.ds(row - cx, 8), :][:, k : k + 1]
                        v = pltpu.roll(v, 1 if cy == 1 else 127, 1)
                        v = jnp.where(lane == (0 if cy == 1 else 127), h, v)
                    pieces.append(v)
            res.append(join(*pieces))
        return res

    def streamed_strip(get, orient, z):
        res = []
        for q in range(Q):
            cx, cy, cz = (orient * c for c in VEL[q])
            v = get(q, (z - cz) % 2)
            if cy:
                v = pltpu.roll(v, cy % 8, 0)
            if cx:
                v = pltpu.roll(v, cx % 256, 1)
            res.append(v)
        return res

    def to_halo(get, halo, orient):
        for q in SIDE:
            j = 1 if orient * VEL[q][1] == 1 else 6
            for z in range(2):
                flip[pl.ds(PLACE[q] * 2 + z, 1), :] = get(q, z, j)
        low = flip[:, :128].T
        high = flip[:, 128:].T
        halo[pl.ds(8, 128), :] = low
        outer = jnp.where(row8 < 4, high[0:8], high[120:128])
        halo[pl.ds(136, 8), :] = outer
        halo[pl.ds(0, 8), :] = outer
        halo[pl.ds(144, 8), :] = low[0:8]

    def put(ref, rows, values):
        for q in range(Q):
            for i, row in enumerate(rows):
                for z in range(2):
                    at = i * 256 + z * 128
                    ref[q, z, pl.ds(row, 8), :] = values[q][:, at : at + 128]

    def put_outer(ref, side, values):
        for q in range(Q):
            for z in range(2):
                ref[q, z, pl.ds(136, 8), :] = values[q][:, z * 128 : z * 128 + 128]
                ref[q, z, pl.ds(0, 8), :] = values[q][:, z * 128 : z * 128 + 128]
                ref[q, z, pl.ds(144, 8), :] = ref[q, z, pl.ds(8, 8), :]
                side[z, q] = values[q][:, 256 + z * 256 : 512 + z * 256]

    def block(ref, rows):
        return [join(*[ref[q, z, pl.ds(r, 8), :] for r in rows for z in range(2)]) for q in range(Q)]

    def solid_at(rows):
        return join(*[mask[z, pl.ds(r, 8), :] for r in rows for z in range(2)]) > 0

    outer_solid = join(line_of(38), line_of(39), strip_of(38), strip_of(39)) > 0.5

    def rows_of(b, offset):
        return [pl.multiple_of((b + w * STEPS) * 8, 8) + offset for w in range(WIDE)]

    def first(b, carry):
        put(post, rows_of(b, 8), collide(block(dist, rows_of(b, 0)), solid_at(rows_of(b, 0)), b))
        return carry

    lax.fori_loop(0, STEPS, first, 0)
    d = [
        join(line_of(2 * q), line_of(2 * q + 1), strip_of(2 * q), strip_of(2 * q + 1)) for q in range(Q)
    ]
    put_outer(post, spost, collide(d, outer_solid, None))
    to_halo(lambda q, z, j: spost[z, q, pl.ds(j, 1), :], hpost, 1)
    to_halo(
        lambda q, z, j: join(
            strip[0, pl.ds(j * IDX + 40 + 2 * q + z, 1), :], strip[1, pl.ds(j * IDX + 40 + 2 * q + z, 1), :]
        ),
        hcot,
        -1,
    )

    def second(b, carry):
        u = streamed(post, hpost, rows_of(b, 8), 1)
        g = streamed(gpad, hcot, rows_of(b, 8), -1)
        put(gmid, rows_of(b, 8), backward(u, g, solid_at(rows_of(b, 0)), None, True))
        return carry

    lax.fori_loop(0, STEPS, second, 0)
    us = [streamed(post, hpost, [136], 1)] + [
        streamed_strip(lambda q, zs: spost[zs, q], 1, z) for z in range(2)
    ]
    gs = [streamed(gpad, hcot, [136], -1)] + [
        streamed_strip(lambda q, zs: strip_of(40 + 2 * q + zs), -1, z) for z in range(2)
    ]
    u = [join(*[v[q] for v in us]) for q in range(Q)]
    g = [join(*[v[q] for v in gs]) for q in range(Q)]
    put_outer(gmid, smid, backward(u, g, outer_solid, None, False))
    to_halo(lambda q, z, j: smid[z, q, pl.ds(j, 1), :], hmid, -1)

    def third(b, carry):
        g = streamed(gmid, hmid, rows_of(b, 8), -1)
        rows = rows_of(b, 0)
        put(out, rows, backward(block(dist, rows), g, solid_at(rows), hid[b], True))
        return carry

    lax.fori_loop(0, STEPS, third, 0)
    parts[pl.ds(0, 20), :] = acc_in[...].T[:20]
    parts[pl.ds(20, 20), :] = acc_out[pl.ds(0, 20), :]
    flip[...] = jnp.zeros_like(flip)
    for q in range(Q):
        flip[pl.ds(q, 1), :128] = jnp.sum(accb[pl.ds(q * 8, 8), :], axis=0, keepdims=True)
    parts[pl.ds(40, 8), :] = jnp.broadcast_to(jnp.sum(flip[:, :128].T, axis=0, keepdims=True), (8, 128))


def main_call(*args):
    field = pltpu.VMEM((Q, 2, 152, 128), f32)
    halo = pltpu.VMEM((152, 128), f32)
    return pl.pallas_call(
        main_kernel,
        out_shape=[jax.ShapeDtypeStruct((Q, 2, 128, 128), f32), jax.ShapeDtypeStruct((48, 128), f32)],
        in_specs=vmem(len(args)),
        out_specs=vmem(2),
        scratch_shapes=[
            field, field, field,
            pltpu.VMEM((STEPS, 1024, 256 * WIDE), f32),
            halo, halo, halo,
            pltpu.VMEM((2, 640, 128), f32),
            pltpu.VMEM((2, Q, 8, 256), f32),
            pltpu.VMEM((2, Q, 8, 256), f32),
            pltpu.VMEM((128, 256), f32),
            pltpu.VMEM((2 * WIDE, 432, 128), f32),
            pltpu.VMEM((128, 128), f32),
            pltpu.VMEM((32, 128), f32),
            pltpu.VMEM((152, 128), f32),
        ],
        compiler_params=pltpu.CompilerParams(vmem_limit_bytes=58 * 2**20),
    )(*args)


def neighbours(axis):
    size = lax.axis_size(axis)
    up = [(i, (i + 1) % size) for i in range(size)]
    return up, [(j, i) for i, j in up]


def summed(values):
    nx, ny = lax.axis_size("gx"), lax.axis_size("gy")

    def from_partner(values, partner):
        pairs = []
        for x in range(nx):
            for y in range(ny):
                px, py = partner(x, y)
                pairs.append((x * ny + y, px * ny + py))
        return lax.ppermute(values, ("gx", "gy"), pairs)

    if (nx, ny) != (8, 16):
        for k in range(nx.bit_length() - 1):
            values = values + from_partner(values, lambda x, y: (x ^ (1 << k), y))
        for k in range(ny.bit_length() - 1):
            values = values + from_partner(values, lambda x, y: (x, y ^ (1 << k)))
        return values
    got = [values] + [
        from_partner(values, lambda x, y: (x ^ ((d >> 1) & 1), y ^ (d & 1) ^ (((d >> 2) & 1) << 1))) for d in range(1, 8)
    ]
    while len(got) > 1:
        got = [got[i] + got[i + 1] for i in range(0, len(got), 2)]
    copies = jnp.broadcast_to(got[0][None], (4,) + values.shape)
    groups = [[2 * y + low for y in range(4)] for low in range(2)]
    values = lax.all_to_all(copies, "gx", 0, 0, tiled=True, axis_index_groups=groups)
    values = (values[0] + values[1]) + (values[2] + values[3])
    other = (3, 2, 1, 0)
    values = values + from_partner(values, lambda x, y: (x, y ^ 4))
    return values + from_partner(values, lambda x, y: (x, other[y // 4] * 4 + y % 4))


def shards(dist, cot, mask, weight_in, bias_in, weight_out, bias_out):
    send_up, send_down, cols = pack(dist, cot, mask)
    up, down = neighbours("gx")
    from_up = lax.ppermute(send_up, "gx", up)
    from_down = lax.ppermute(send_down, "gx", down)
    nets = make_weights(weight_in, weight_out, bias_in, bias_out)
    side_up, side_down, edge, lines = corners(from_up, from_down, cols)
    up, down = neighbours("gy")
    from_left = lax.ppermute(side_up, "gy", up)
    from_right = lax.ppermute(side_down, "gy", down)
    grad, parts = main_call(dist, cot, mask, cols, edge, from_left, from_right, lines, *nets)
    total = summed(parts)
    cells = mask.size * lax.axis_size("gx") * lax.axis_size("gy")
    total = total * (1.0 / math.sqrt(cells))
    return grad, total[:19], total[19], total[20:39].T, total[40, :19]


def solution(mesh):
    field = P(None, None, "gx", "gy")
    return jax.shard_map(
        shards,
        mesh=mesh,
        in_specs=(field, field, P(None, "gx", "gy"), P(), P(), P(), P()),
        out_specs=(field, P(), P(), P(), P()),
        check_vma=False,
    )
```

```python
import functools
import math

import jax
import jax.numpy as jnp
from jax import lax
from jax.experimental import pallas as pl
from jax.experimental.pallas import tpu as pltpu
from jax.sharding import PartitionSpec as P

VEL = (
    (0, 0, 0), (1, 0, 0), (-1, 0, 0), (0, 1, 0), (0, -1, 0), (0, 0, 1), (0, 0, -1),
    (1, 1, 0), (-1, -1, 0), (1, -1, 0), (-1, 1, 0), (1, 0, 1), (-1, 0, -1), (1, 0, -1),
    (-1, 0, 1), (0, 1, 1), (0, -1, -1), (0, 1, -1), (0, -1, 1),
)
OPP = (0, 2, 1, 4, 3, 6, 5, 8, 7, 10, 9, 12, 11, 14, 13, 16, 15, 18, 17)
Q = 19
WIDE = 4
STEPS = 16 // WIDE
SIDE = tuple(q for q in range(Q) if VEL[q][1])
PLACE = {q: i for i, q in enumerate(SIDE)}
f32 = jnp.float32
bf16 = jnp.bfloat16
NT = (((1,), (1,)), ((), ()))
IDX = 80
COLS = (126, 127, 0, 0, 127, 127, 0, 1)


def iota(shape, dim):
    return lax.broadcasted_iota(jnp.int32, shape, dim)


def vmem(n):
    return [pl.BlockSpec(memory_space=pltpu.VMEM)] * n


def weights_kernel(win, wtout, bias, bias_out, a_in, a_out, b_out, b_in, bias_rows):
    TN = (((0,), (0,)), ((), ()))
    rep = jnp.where(iota((Q, 160), 1) // 8 == iota((Q, 160), 0), 1.0, 0.0).astype(bf16)
    rept = jnp.where(iota((160, Q), 0) // 8 == iota((160, Q), 1), 1.0, 0.0).astype(bf16)
    wide_in = lax.dot_general(win[...], rep, TN, preferred_element_type=f32)
    wide_out = lax.dot_general(wtout[...], rep, TN, preferred_element_type=f32)
    tall_out = jnp.dot(rept, wtout[...], preferred_element_type=f32)
    tall_in = jnp.dot(rept, win[...], preferred_element_type=f32)
    b = jnp.broadcast_to(bias[...], (128, 128)).T
    b = jnp.concatenate([b, b[:, :32]], axis=1)
    high = b.astype(bf16).astype(f32)
    mid = (b - high).astype(bf16).astype(f32)
    low = b - high - mid
    col = iota((128, 160), 1)
    row = iota((160, 128), 0)
    biased = jnp.where(col == 152, high, jnp.where(col == 153, mid, jnp.where(col == 154, low, 0.0)))
    for k in range(8):
        own = (col % 8 == k) & (col < 152)
        own_row = (row % 8 == k) & (row < 152)
        part = slice(k * 128, k * 128 + 128)
        a_in[part, :] = jnp.where(own, wide_in, biased).astype(bf16)
        a_out[part, :] = jnp.where(own, wide_out, 0.0).astype(bf16)
        b_out[:, part] = jnp.where(own_row, tall_out, 0.0).astype(bf16)
        b_in[:, part] = jnp.where(own_row, tall_in, 0.0).astype(bf16)
    for q in range(Q):
        bias_rows[pl.ds(q * 8, 8), :] = jnp.broadcast_to(bias_out[0:1, q : q + 1], (8, 128))


def make_weights(weight_in, weight_out, bias_in, bias_out):
    return pl.pallas_call(
        weights_kernel,
        out_shape=[jax.ShapeDtypeStruct((1024, 160), bf16)] * 2
        + [jax.ShapeDtypeStruct((160, 1024), bf16)] * 2
        + [jax.ShapeDtypeStruct((152, 128), f32)],
        in_specs=vmem(4),
        out_specs=vmem(5),
        cost_estimate=pl.CostEstimate(flops=10**8, bytes_accessed=2 * 10**6, transcendentals=0),
    )(weight_in, weight_out.T, bias_in[None], bias_out[None])


def pack_kernel(dist, cot, mask, up, down, cols, line):
    for out, rows in ((up, (126, 127)), (down, (0, 1))):
        for i, r in enumerate(rows):
            line[pl.ds(0, 38), :] = dist[pl.ds(r, 38, stride=128), :]
            line[pl.ds(38, 2), :] = mask[pl.ds(r, 2, stride=128), :].astype(f32)
            line[pl.ds(40, 38), :] = cot[pl.ds(r, 38, stride=128), :]
            line[pl.ds(78, 2), :] = jnp.zeros((2, 128), f32)
            out[pl.ds(i * 80, 80), :] = line[...].astype(bf16)
    lane, row = iota((8, 128), 1), iota((8, 128), 0)
    pick = jnp.zeros((8, 128), f32)
    for j, y in enumerate(COLS):
        pick = jnp.where((row == j) & (lane == y), 1.0, pick)
    pick = pick.astype(bf16)

    def slabs(ref, first, count, place):
        values = ref[pl.ds(first * 128, count * 128), :].astype(f32).astype(bf16)
        got = lax.dot_general(pick, values, NT, preferred_element_type=f32)
        for i in range(count):
            cols[pl.ds(place + i, 8, stride=IDX), :] = got[:, i * 128 : i * 128 + 128]

    for half in range(2):
        slabs(dist, half * 19, 19, half * 19)
        slabs(cot, half * 19, 19, 40 + half * 19)
    slabs(mask, 0, 2, 38)
    for z in range(2):
        cols[pl.ds(78 + z, 8, stride=IDX), :] = jnp.zeros((8, 128), f32)


def pack(dist, cot, mask):
    return pl.pallas_call(
        pack_kernel,
        out_shape=[jax.ShapeDtypeStruct((160, 128), bf16)] * 2 + [jax.ShapeDtypeStruct((640, 128), f32)],
        in_specs=vmem(3),
        out_specs=vmem(3),
        scratch_shapes=[pltpu.VMEM((80, 128), f32)],
    )(dist.reshape(38 * 128, 128), cot.reshape(38 * 128, 128), mask.reshape(256, 128))


def corner_kernel(from_up, from_down, cols, send_up, send_down, edge, lines):
    sides = ((from_down, 0, 0), (from_down, 1, 1), (from_up, 0, 126), (from_up, 1, 127))
    lane = iota((80, 128), 1)
    got = [ref[pl.ds(i * 80, 80), :].astype(f32) for ref, i, _ in sides]
    for (_, _, place), values in zip(sides, got):
        lines[pl.ds(place % 8, 80, stride=8), :] = values
    for r in range(2, 6):
        lines[pl.ds(r, 80, stride=8), :] = jnp.zeros((80, 128), f32)
    for j, y in enumerate(COLS):
        out = jnp.zeros((80, 128), f32)
        for (_, _, place), values in zip(sides, got):
            out = jnp.where(lane == place, values[:, y : y + 1], out)
        edge[pl.ds(j * 80, 80), :] = out
    for out, first in ((send_up, 0), (send_down, 6)):
        out[:, :128] = cols[pl.ds(first * 80, 160), :].astype(bf16)
        out[:, 128:] = edge[pl.ds(first * 80, 160), :].astype(bf16)


def corners(from_up, from_down, cols):
    return pl.pallas_call(
        corner_kernel,
        out_shape=[jax.ShapeDtypeStruct((160, 256), bf16)] * 2
        + [jax.ShapeDtypeStruct((640, 128), f32)] * 2,
        in_specs=vmem(3),
        out_specs=vmem(4),
    )(from_up, from_down, cols)


def main_kernel(
    dist_far, cot_far, mask, cols, edge, from_left, from_right, lines,
    a_in, a_out, b_out, b_in, bias_out,
    out_far, parts,
    dist, out, in_sem, cot_sem, out_sem, post, gmid, gpad, hid, hpost, hcot, hmid, strip, spost, smid, flip, uo, acc_in, acc_out, accb,
):
    lane = iota((8, 128), 1)
    row8 = iota((8, 128), 0)

    def join(*parts):
        return jnp.concatenate(parts, axis=1)

    def rows_of(b, offset):
        return [pl.multiple_of((b + w * STEPS) * 8, 8) + offset for w in range(WIDE)]

    def in_copies(b):
        return [
            pltpu.make_async_copy(
                dist_far.at[:, :, pl.ds(r, 8), :], dist.at[:, :, pl.ds(r, 8), :], in_sem.at[b * WIDE + w]
            )
            for w, r in enumerate(rows_of(b, 0))
        ]

    def out_copies(b):
        return [
            pltpu.make_async_copy(
                out.at[:, :, pl.ds(r, 8), :], out_far.at[:, :, pl.ds(r, 8), :], out_sem.at[b * WIDE + w]
            )
            for w, r in enumerate(rows_of(b, 0))
        ]

    for b in range(STEPS):
        for copy in in_copies(b):
            copy.start()
    cot_copy = pltpu.make_async_copy(cot_far, gpad.at[:, :, pl.ds(8, 128), :], cot_sem)
    cot_copy.start()

    strip[0] = cols[...]
    strip[1] = edge[...]
    strip[0, pl.ds(0, 160), :] = from_left[:, :128].astype(f32)
    strip[1, pl.ds(0, 160), :] = from_left[:, 128:].astype(f32)
    strip[0, pl.ds(480, 160), :] = from_right[:, :128].astype(f32)
    strip[1, pl.ds(480, 160), :] = from_right[:, 128:].astype(f32)

    def strip_of(i):
        return join(strip[0, pl.ds(i, 8, stride=IDX), :], strip[1, pl.ds(i, 8, stride=IDX), :])

    def line_of(i):
        return lines[pl.ds(i * 8, 8), :]

    uo[...] = jnp.zeros_like(uo)
    uo[:, pl.ds(19 * 9, 9), :] = jnp.ones((2 * WIDE, 9, 128), f32)
    acc_in[...] = jnp.zeros_like(acc_in)
    acc_out[...] = jnp.zeros_like(acc_out)
    accb[...] = jnp.zeros_like(accb)
    flip[...] = jnp.zeros_like(flip)

    def operand(values):
        ones = jnp.ones(values[0].shape, f32)
        return jnp.concatenate(values + [ones], axis=0).astype(bf16)

    def hidden(values):
        return jnp.tanh(jnp.dot(a_in[...], operand(values), preferred_element_type=f32))

    def collide(d, solid, keep):
        t = hidden(d)
        if keep is not None:
            hid[keep] = t
        o = jnp.dot(b_out[...], t.astype(bf16), preferred_element_type=f32)
        res = []
        for q in range(Q):
            bias = bias_out[pl.ds(q * 8, 8), :]
            val = d[q] + o[q * 8 : q * 8 + 8] + join(*[bias] * (d[q].shape[1] // 128))
            val = jnp.where(solid, d[OPP[q]], val)
            res.append(val.astype(bf16).astype(f32))
        return res

    def backward(u, g, solid, t, partial):
        og = [jnp.where(solid, 0.0, v) for v in g]
        if t is None:
            t = hidden(u)
        hg = jnp.dot(a_out[...], operand(og), preferred_element_type=f32)
        hb = (hg * (1.0 - t * t)).astype(bf16)
        ig = jnp.dot(b_in[...], hb, preferred_element_type=f32)
        if partial:
            act = t.astype(bf16)
            halves = [slice(h * 128, h * 128 + 128) for h in range(2 * WIDE)]
            for q in range(Q):
                for h, part in enumerate(halves):
                    uo[h, pl.ds(q * 9, 8), :] = u[q][:, part]
                    uo[h, pl.ds(216 + q * 9, 8), :] = og[q][:, part]
                accb[pl.ds(q * 8, 8), :] += sum(og[q][:, part] for part in halves)

            def cells(first):
                lines24 = join(
                    *[uo[h, pl.ds(first + k, 24, stride=9), :] for k in range(8) for h in range(2 * WIDE)]
                )
                return jnp.concatenate([lines24, jnp.zeros((8, lines24.shape[1]), f32)], axis=0).astype(bf16)

            def units(values):
                return join(*[values[k * 128 : k * 128 + 128] for k in range(8)])

            left = jnp.concatenate([units(hb), cells(216)], axis=0)
            right = jnp.concatenate([units(act), cells(0)], axis=0)
            both = lax.dot_general(left, right, NT, preferred_element_type=f32)
            acc_in[:, :32] += both[:128, 128:]
            acc_out[...] += both[128:, :128]
        return [
            og[q] + ig[q * 8 : q * 8 + 8] + jnp.where(solid, g[OPP[q]], 0.0) for q in range(Q)
        ]

    def streamed(ref, halo, rows, orient):
        res = []
        for q in range(Q):
            cx, cy, cz = (orient * c for c in VEL[q])
            pieces = []
            for row in rows:
                for z in range(2):
                    zs = (z - cz) % 2
                    v = ref[q, zs, pl.ds(row - cx, 8), :]
                    if cy:
                        k = PLACE[q] * 2 + zs
                        h = halo[pl.ds(row - cx, 8), :][:, k : k + 1]
                        v = pltpu.roll(v, 1 if cy == 1 else 127, 1)
                        v = jnp.where(lane == (0 if cy == 1 else 127), h, v)
                    pieces.append(v)
            res.append(join(*pieces))
        return res

    def streamed_strip(get, orient, z):
        res = []
        for q in range(Q):
            cx, cy, cz = (orient * c for c in VEL[q])
            v = get(q, (z - cz) % 2)
            if cy:
                v = pltpu.roll(v, cy % 8, 0)
            if cx:
                v = pltpu.roll(v, cx % 256, 1)
            res.append(v)
        return res

    def to_halo(get, halo, orient):
        for q in SIDE:
            j = 1 if orient * VEL[q][1] == 1 else 6
            for z in range(2):
                flip[pl.ds(PLACE[q] * 2 + z, 1), :] = get(q, z, j)
        low = flip[:, :128].T
        high = flip[:, 128:].T
        halo[pl.ds(8, 128), :] = low
        outer = jnp.where(row8 < 4, high[0:8], high[120:128])
        halo[pl.ds(136, 8), :] = outer
        halo[pl.ds(0, 8), :] = outer
        halo[pl.ds(144, 8), :] = low[0:8]

    def put(ref, rows, values):
        for q in range(Q):
            for i, row in enumerate(rows):
                for z in range(2):
                    at = i * 256 + z * 128
                    ref[q, z, pl.ds(row, 8), :] = values[q][:, at : at + 128]

    def put_outer(ref, side, values):
        for q in range(Q):
            for z in range(2):
                ref[q, z, pl.ds(136, 8), :] = values[q][:, z * 128 : z * 128 + 128]
                ref[q, z, pl.ds(0, 8), :] = values[q][:, z * 128 : z * 128 + 128]
                ref[q, z, pl.ds(144, 8), :] = ref[q, z, pl.ds(8, 8), :]
                side[z, q] = values[q][:, 256 + z * 256 : 512 + z * 256]

    def block(ref, rows):
        return [join(*[ref[q, z, pl.ds(r, 8), :] for r in rows for z in range(2)]) for q in range(Q)]

    def solid_at(rows):
        return join(*[mask[z, pl.ds(r, 8), :] for r in rows for z in range(2)]) > 0

    outer_solid = join(line_of(38), line_of(39), strip_of(38), strip_of(39)) > 0.5

    def first(b, carry):
        for copy in in_copies(b):
            copy.wait()
        put(post, rows_of(b, 8), collide(block(dist, rows_of(b, 0)), solid_at(rows_of(b, 0)), b))
        return carry

    lax.fori_loop(0, STEPS, first, 0)
    d = [
        join(line_of(2 * q), line_of(2 * q + 1), strip_of(2 * q), strip_of(2 * q + 1)) for q in range(Q)
    ]
    put_outer(post, spost, collide(d, outer_solid, None))
    to_halo(lambda q, z, j: spost[z, q, pl.ds(j, 1), :], hpost, 1)
    to_halo(
        lambda q, z, j: join(
            strip[0, pl.ds(j * IDX + 40 + 2 * q + z, 1), :], strip[1, pl.ds(j * IDX + 40 + 2 * q + z, 1), :]
        ),
        hcot,
        -1,
    )

    cot_copy.wait()
    for q in range(Q):
        for z in range(2):
            halo = line_of(40 + 2 * q + z)
            gpad[q, z, pl.ds(0, 8), :] = halo
            gpad[q, z, pl.ds(136, 8), :] = halo
            gpad[q, z, pl.ds(144, 8), :] = gpad[q, z, pl.ds(8, 8), :]

    def second(b, carry):
        u = streamed(post, hpost, rows_of(b, 8), 1)
        g = streamed(gpad, hcot, rows_of(b, 8), -1)
        put(gmid, rows_of(b, 8), backward(u, g, solid_at(rows_of(b, 0)), None, True))
        return carry

    lax.fori_loop(0, STEPS, second, 0)
    us = [streamed(post, hpost, [136], 1)] + [
        streamed_strip(lambda q, zs: spost[zs, q], 1, z) for z in range(2)
    ]
    gs = [streamed(gpad, hcot, [136], -1)] + [
        streamed_strip(lambda q, zs: strip_of(40 + 2 * q + zs), -1, z) for z in range(2)
    ]
    u = [join(*[v[q] for v in us]) for q in range(Q)]
    g = [join(*[v[q] for v in gs]) for q in range(Q)]
    put_outer(gmid, smid, backward(u, g, outer_solid, None, False))
    to_halo(lambda q, z, j: smid[z, q, pl.ds(j, 1), :], hmid, -1)

    def third(b, carry):
        g = streamed(gmid, hmid, rows_of(b, 8), -1)
        rows = rows_of(b, 0)
        put(out, rows, backward(block(dist, rows), g, solid_at(rows), hid[b], True))
        for copy in out_copies(b):
            copy.start()
        return carry

    lax.fori_loop(0, STEPS, third, 0)
    for b in range(STEPS):
        for copy in out_copies(b):
            copy.wait()
    flip[...] = jnp.zeros_like(flip)
    flip[pl.ds(20, 20), :128] = acc_out[pl.ds(0, 20), :]
    for q in range(Q):
        flip[pl.ds(q, 1), 128:] = jnp.sum(accb[pl.ds(q * 8, 8), :], axis=0, keepdims=True)
    own = acc_in[...]
    lane128 = iota((128, 128), 1)
    biases = jnp.broadcast_to(jnp.sum(flip[:, 128:], axis=1, keepdims=True), (128, 128))
    own = jnp.where(lane128 < 20, own, jnp.where(lane128 == 40, biases, flip[:, :128].T))
    parts[...] = own[:, :48]


def main_call(*args):
    field = pltpu.VMEM((Q, 2, 152, 128), f32)
    halo = pltpu.VMEM((152, 128), f32)
    return pl.pallas_call(
        main_kernel,
        out_shape=[jax.ShapeDtypeStruct((Q, 2, 128, 128), f32), jax.ShapeDtypeStruct((128, 48), f32)],
        in_specs=[pl.BlockSpec(memory_space=pl.ANY)] * 2 + vmem(len(args) - 2),
        out_specs=[pl.BlockSpec(memory_space=pl.ANY)] + vmem(1),
        scratch_shapes=[
            pltpu.VMEM((Q, 2, 128, 128), f32),
            pltpu.VMEM((Q, 2, 128, 128), f32),
            pltpu.SemaphoreType.DMA((16,)),
            pltpu.SemaphoreType.DMA,
            pltpu.SemaphoreType.DMA((16,)),
            field, field, field,
            pltpu.VMEM((STEPS, 1024, 256 * WIDE), f32),
            halo, halo, halo,
            pltpu.VMEM((2, 640, 128), f32),
            pltpu.VMEM((2, Q, 8, 256), f32),
            pltpu.VMEM((2, Q, 8, 256), f32),
            pltpu.VMEM((128, 256), f32),
            pltpu.VMEM((2 * WIDE, 432, 128), f32),
            pltpu.VMEM((128, 128), f32),
            pltpu.VMEM((32, 128), f32),
            pltpu.VMEM((152, 128), f32),
        ],
        compiler_params=pltpu.CompilerParams(vmem_limit_bytes=58 * 2**20),
    )(*args)


def neighbours(axis):
    size = lax.axis_size(axis)
    up = [(i, (i + 1) % size) for i in range(size)]
    return up, [(j, i) for i, j in up]


def summed(values):
    axes = ("gx", "gy")
    count = lax.axis_size("gx") * lax.axis_size("gy")
    rows = values.shape[0] // count
    got = lax.all_to_all(values, axes, 0, 0, tiled=True)
    mine = jnp.sum(got.reshape(count, rows, values.shape[1]), axis=0)
    return lax.all_to_all(jnp.tile(mine, (count, 1)), axes, 0, 0, tiled=True)


def finish_kernel(factor, total, d_in, d_bias_in, d_out, d_bias_out):
    wide = jnp.concatenate([total[...], jnp.zeros((128, 80), f32)], axis=1)
    rows = wide.T * factor
    d_in[...] = rows[:19]
    d_bias_in[...] = rows[19:20]
    d_out[...] = rows[20:39]
    d_bias_out[...] = rows[40:41, :19]


def finish(total, factor):
    return pl.pallas_call(
        functools.partial(finish_kernel, factor),
        out_shape=[jax.ShapeDtypeStruct(s, f32) for s in ((19, 128), (1, 128), (19, 128), (1, 19))],
        in_specs=vmem(1),
        out_specs=vmem(4),
    )(total)


def shards(dist, cot, mask, weight_in, bias_in, weight_out, bias_out):
    send_up, send_down, cols = pack(dist, cot, mask)
    up, down = neighbours("gx")
    from_up = lax.ppermute(send_up, "gx", up)
    from_down = lax.ppermute(send_down, "gx", down)
    nets = make_weights(weight_in, weight_out, bias_in, bias_out)
    side_up, side_down, edge, lines = corners(from_up, from_down, cols)
    up, down = neighbours("gy")
    from_left = lax.ppermute(side_up, "gy", up)
    from_right = lax.ppermute(side_down, "gy", down)
    grad, parts = main_call(dist, cot, mask, cols, edge, from_left, from_right, lines, *nets)
    total = summed(parts)
    cells = mask.size * lax.axis_size("gx") * lax.axis_size("gy")
    d_in, d_bias_in, d_out, d_bias_out = finish(total, 1.0 / math.sqrt(cells))
    return grad, d_in, d_bias_in[0], d_out.T, d_bias_out[0]


def solution(mesh):
    field = P(None, None, "gx", "gy")
    return jax.shard_map(
        shards,
        mesh=mesh,
        in_specs=(field, field, P(None, "gx", "gy"), P(), P(), P(), P()),
        out_specs=(field, P(), P(), P(), P()),
        check_vma=False,
    )
```

```python
import math

import jax
import jax.numpy as jnp
from jax import lax
from jax.experimental import pallas as pl
from jax.experimental.pallas import tpu as pltpu
from jax.sharding import PartitionSpec as P

VEL = (
    (0, 0, 0), (1, 0, 0), (-1, 0, 0), (0, 1, 0), (0, -1, 0), (0, 0, 1), (0, 0, -1),
    (1, 1, 0), (-1, -1, 0), (1, -1, 0), (-1, 1, 0), (1, 0, 1), (-1, 0, -1), (1, 0, -1),
    (-1, 0, 1), (0, 1, 1), (0, -1, -1), (0, 1, -1), (0, -1, 1),
)
OPP = (0, 2, 1, 4, 3, 6, 5, 8, 7, 10, 9, 12, 11, 14, 13, 16, 15, 18, 17)
Q = 19
WIDE = 8
STEPS = 16 // WIDE
SIDE = tuple(q for q in range(Q) if VEL[q][1])
PLACE = {q: i for i, q in enumerate(SIDE)}
f32 = jnp.float32
bf16 = jnp.bfloat16
NT = (((1,), (1,)), ((), ()))
IDX = 80
COLS = (126, 127, 0, 0, 127, 127, 0, 1)


def iota(shape, dim):
    return lax.broadcasted_iota(jnp.int32, shape, dim)


def vmem(n):
    return [pl.BlockSpec(memory_space=pltpu.VMEM)] * n


def weights_kernel(win, wtout, bias, bias_out, a_in, a_out, b_out, b_in, bias_rows):
    TN = (((0,), (0,)), ((), ()))
    rep = jnp.where(iota((Q, 160), 1) // 8 == iota((Q, 160), 0), 1.0, 0.0).astype(bf16)
    rept = jnp.where(iota((160, Q), 0) // 8 == iota((160, Q), 1), 1.0, 0.0).astype(bf16)
    wide_in = lax.dot_general(win[...], rep, TN, preferred_element_type=f32)
    wide_out = lax.dot_general(wtout[...], rep, TN, preferred_element_type=f32)
    tall_out = jnp.dot(rept, wtout[...], preferred_element_type=f32)
    tall_in = jnp.dot(rept, win[...], preferred_element_type=f32)
    b = jnp.broadcast_to(bias[...], (128, 128)).T
    b = jnp.concatenate([b, b[:, :32]], axis=1)
    high = b.astype(bf16).astype(f32)
    mid = (b - high).astype(bf16).astype(f32)
    low = b - high - mid
    col = iota((128, 160), 1)
    row = iota((160, 128), 0)
    biased = jnp.where(col == 152, high, jnp.where(col == 153, mid, jnp.where(col == 154, low, 0.0)))
    for k in range(8):
        own = (col % 8 == k) & (col < 152)
        own_row = (row % 8 == k) & (row < 152)
        part = slice(k * 128, k * 128 + 128)
        a_in[part, :] = jnp.where(own, wide_in, biased).astype(bf16)
        a_out[part, :] = jnp.where(own, wide_out, 0.0).astype(bf16)
        b_out[:, part] = jnp.where(own_row, tall_out, 0.0).astype(bf16)
        b_in[:, part] = jnp.where(own_row, tall_in, 0.0).astype(bf16)
    for q in range(Q):
        bias_rows[pl.ds(q * 8, 8), :] = jnp.broadcast_to(bias_out[0:1, q : q + 1], (8, 128))


def make_weights(weight_in, weight_out, bias_in, bias_out):
    return pl.pallas_call(
        weights_kernel,
        out_shape=[jax.ShapeDtypeStruct((1024, 160), bf16)] * 2
        + [jax.ShapeDtypeStruct((160, 1024), bf16)] * 2
        + [jax.ShapeDtypeStruct((152, 128), f32)],
        in_specs=vmem(4),
        out_specs=vmem(5),
        cost_estimate=pl.CostEstimate(flops=10**8, bytes_accessed=2 * 10**6, transcendentals=0),
    )(weight_in, weight_out.T, bias_in[None], bias_out[None])


def pack_kernel(dist, cot, mask, up, down, cols, line):
    for out, rows in ((up, (126, 127)), (down, (0, 1))):
        for i, r in enumerate(rows):
            line[pl.ds(0, 38), :] = dist[pl.ds(r, 38, stride=128), :]
            line[pl.ds(38, 2), :] = mask[pl.ds(r, 2, stride=128), :].astype(f32)
            line[pl.ds(40, 38), :] = cot[pl.ds(r, 38, stride=128), :]
            line[pl.ds(78, 2), :] = jnp.zeros((2, 128), f32)
            out[pl.ds(i * 80, 80), :] = line[...].astype(bf16)
    lane, row = iota((8, 128), 1), iota((8, 128), 0)
    pick = jnp.zeros((8, 128), f32)
    for j, y in enumerate(COLS):
        pick = jnp.where((row == j) & (lane == y), 1.0, pick)
    pick = pick.astype(bf16)

    def slabs(ref, first, count, place):
        values = ref[pl.ds(first * 128, count * 128), :].astype(f32).astype(bf16)
        got = lax.dot_general(pick, values, NT, preferred_element_type=f32)
        for i in range(count):
            cols[pl.ds(place + i, 8, stride=IDX), :] = got[:, i * 128 : i * 128 + 128]

    for half in range(2):
        slabs(dist, half * 19, 19, half * 19)
        slabs(cot, half * 19, 19, 40 + half * 19)
    slabs(mask, 0, 2, 38)
    for z in range(2):
        cols[pl.ds(78 + z, 8, stride=IDX), :] = jnp.zeros((8, 128), f32)


def pack(dist, cot, mask):
    return pl.pallas_call(
        pack_kernel,
        out_shape=[jax.ShapeDtypeStruct((160, 128), bf16)] * 2 + [jax.ShapeDtypeStruct((640, 128), f32)],
        in_specs=vmem(3),
        out_specs=vmem(3),
        scratch_shapes=[pltpu.VMEM((80, 128), f32)],
    )(dist.reshape(38 * 128, 128), cot.reshape(38 * 128, 128), mask.reshape(256, 128))


def corner_kernel(from_up, from_down, cols, send_up, send_down, edge, lines):
    sides = ((from_down, 0, 0), (from_down, 1, 1), (from_up, 0, 126), (from_up, 1, 127))
    lane = iota((80, 128), 1)
    got = [ref[pl.ds(i * 80, 80), :].astype(f32) for ref, i, _ in sides]
    for (_, _, place), values in zip(sides, got):
        lines[pl.ds(place % 8, 80, stride=8), :] = values
    for r in range(2, 6):
        lines[pl.ds(r, 80, stride=8), :] = jnp.zeros((80, 128), f32)
    for j, y in enumerate(COLS):
        out = jnp.zeros((80, 128), f32)
        for (_, _, place), values in zip(sides, got):
            out = jnp.where(lane == place, values[:, y : y + 1], out)
        edge[pl.ds(j * 80, 80), :] = out
    for out, first in ((send_up, 0), (send_down, 6)):
        out[:, :128] = cols[pl.ds(first * 80, 160), :].astype(bf16)
        out[:, 128:] = edge[pl.ds(first * 80, 160), :].astype(bf16)


def corners(from_up, from_down, cols):
    return pl.pallas_call(
        corner_kernel,
        out_shape=[jax.ShapeDtypeStruct((160, 256), bf16)] * 2
        + [jax.ShapeDtypeStruct((640, 128), f32)] * 2,
        in_specs=vmem(3),
        out_specs=vmem(4),
    )(from_up, from_down, cols)


def main_kernel(
    dist, cot, mask, cols, edge, from_left, from_right, lines,
    a_in, a_out, b_out, b_in, bias_out,
    out, parts,
    post, gmid, gpad, hid, hpost, hcot, hmid, strip, spost, smid, flip, uo, acc_in, acc_out, accb,
):
    lane = iota((8, 128), 1)
    row8 = iota((8, 128), 0)

    def join(*parts):
        return jnp.concatenate(parts, axis=1)

    strip[0] = cols[...]
    strip[1] = edge[...]
    strip[0, pl.ds(0, 160), :] = from_left[:, :128].astype(f32)
    strip[1, pl.ds(0, 160), :] = from_left[:, 128:].astype(f32)
    strip[0, pl.ds(480, 160), :] = from_right[:, :128].astype(f32)
    strip[1, pl.ds(480, 160), :] = from_right[:, 128:].astype(f32)

    def strip_of(i):
        return join(strip[0, pl.ds(i, 8, stride=IDX), :], strip[1, pl.ds(i, 8, stride=IDX), :])

    def line_of(i):
        return lines[pl.ds(i * 8, 8), :]

    for q in range(Q):
        for z in range(2):
            i = 2 * q + z
            gpad[q, z, pl.ds(8, 128), :] = cot[q, z]
            halo = line_of(40 + i)
            gpad[q, z, pl.ds(0, 8), :] = halo
            gpad[q, z, pl.ds(136, 8), :] = halo
            gpad[q, z, pl.ds(144, 8), :] = cot[q, z, pl.ds(0, 8), :]

    uo[...] = jnp.zeros_like(uo)
    uo[:, pl.ds(19 * 9, 9), :] = jnp.ones((2 * WIDE, 9, 128), f32)
    acc_in[...] = jnp.zeros_like(acc_in)
    acc_out[...] = jnp.zeros_like(acc_out)
    accb[...] = jnp.zeros_like(accb)
    flip[...] = jnp.zeros_like(flip)

    def operand(values):
        ones = jnp.ones(values[0].shape, f32)
        return jnp.concatenate(values + [ones], axis=0).astype(bf16)

    def hidden(values):
        return jnp.tanh(jnp.dot(a_in[...], operand(values), preferred_element_type=f32))

    def collide(d, solid, keep):
        t = hidden(d)
        if keep is not None:
            hid[keep] = t
        o = jnp.dot(b_out[...], t.astype(bf16), preferred_element_type=f32)
        res = []
        for q in range(Q):
            bias = bias_out[pl.ds(q * 8, 8), :]
            val = d[q] + o[q * 8 : q * 8 + 8] + join(*[bias] * (d[q].shape[1] // 128))
            val = jnp.where(solid, d[OPP[q]], val)
            res.append(val.astype(bf16).astype(f32))
        return res

    def backward(u, g, solid, t, partial):
        og = [jnp.where(solid, 0.0, v) for v in g]
        if t is None:
            t = hidden(u)
        hg = jnp.dot(a_out[...], operand(og), preferred_element_type=f32)
        hb = (hg * (1.0 - t * t)).astype(bf16)
        ig = jnp.dot(b_in[...], hb, preferred_element_type=f32)
        if partial:
            act = t.astype(bf16)
            halves = [slice(h * 128, h * 128 + 128) for h in range(2 * WIDE)]
            for q in range(Q):
                for h, part in enumerate(halves):
                    uo[h, pl.ds(q * 9, 8), :] = u[q][:, part]
                    uo[h, pl.ds(216 + q * 9, 8), :] = og[q][:, part]
                accb[pl.ds(q * 8, 8), :] += sum(og[q][:, part] for part in halves)

            def cells(first):
                lines24 = join(
                    *[uo[h, pl.ds(first + k, 24, stride=9), :] for k in range(8) for h in range(2 * WIDE)]
                )
                return jnp.concatenate([lines24, jnp.zeros((8, lines24.shape[1]), f32)], axis=0).astype(bf16)

            def units(values):
                return join(*[values[k * 128 : k * 128 + 128] for k in range(8)])

            left = jnp.concatenate([units(hb), cells(216)], axis=0)
            right = jnp.concatenate([units(act), cells(0)], axis=0)
            both = lax.dot_general(left, right, NT, preferred_element_type=f32)
            acc_in[:, :32] += both[:128, 128:]
            acc_out[...] += both[128:, :128]
        return [
            og[q] + ig[q * 8 : q * 8 + 8] + jnp.where(solid, g[OPP[q]], 0.0) for q in range(Q)
        ]

    def streamed(ref, halo, rows, orient):
        res = []
        for q in range(Q):
            cx, cy, cz = (orient * c for c in VEL[q])
            pieces = []
            for row in rows:
                for z in range(2):
                    zs = (z - cz) % 2
                    v = ref[q, zs, pl.ds(row - cx, 8), :]
                    if cy:
                        k = PLACE[q] * 2 + zs
                        h = halo[pl.ds(row - cx, 8), :][:, k : k + 1]
                        v = pltpu.roll(v, 1 if cy == 1 else 127, 1)
                        v = jnp.where(lane == (0 if cy == 1 else 127), h, v)
                    pieces.append(v)
            res.append(join(*pieces))
        return res

    def streamed_strip(get, orient, z):
        res = []
        for q in range(Q):
            cx, cy, cz = (orient * c for c in VEL[q])
            v = get(q, (z - cz) % 2)
            if cy:
                v = pltpu.roll(v, cy % 8, 0)
            if cx:
                v = pltpu.roll(v, cx % 256, 1)
            res.append(v)
        return res

    def to_halo(get, halo, orient):
        for q in SIDE:
            j = 1 if orient * VEL[q][1] == 1 else 6
            for z in range(2):
                flip[pl.ds(PLACE[q] * 2 + z, 1), :] = get(q, z, j)
        low = flip[:, :128].T
        high = flip[:, 128:].T
        halo[pl.ds(8, 128), :] = low
        outer = jnp.where(row8 < 4, high[0:8], high[120:128])
        halo[pl.ds(136, 8), :] = outer
        halo[pl.ds(0, 8), :] = outer
        halo[pl.ds(144, 8), :] = low[0:8]

    def put(ref, rows, values):
        for q in range(Q):
            for i, row in enumerate(rows):
                for z in range(2):
                    at = i * 256 + z * 128
                    ref[q, z, pl.ds(row, 8), :] = values[q][:, at : at + 128]

    def put_outer(ref, side, values):
        for q in range(Q):
            for z in range(2):
                ref[q, z, pl.ds(136, 8), :] = values[q][:, z * 128 : z * 128 + 128]
                ref[q, z, pl.ds(0, 8), :] = values[q][:, z * 128 : z * 128 + 128]
                ref[q, z, pl.ds(144, 8), :] = ref[q, z, pl.ds(8, 8), :]
                side[z, q] = values[q][:, 256 + z * 256 : 512 + z * 256]

    def block(ref, rows):
        return [join(*[ref[q, z, pl.ds(r, 8), :] for r in rows for z in range(2)]) for q in range(Q)]

    def solid_at(rows):
        return join(*[mask[z, pl.ds(r, 8), :] for r in rows for z in range(2)]) > 0

    outer_solid = join(line_of(38), line_of(39), strip_of(38), strip_of(39)) > 0.5

    def rows_of(b, offset):
        return [pl.multiple_of((b + w * STEPS) * 8, 8) + offset for w in range(WIDE)]

    def first(b, carry):
        put(post, rows_of(b, 8), collide(block(dist, rows_of(b, 0)), solid_at(rows_of(b, 0)), b))
        return carry

    lax.fori_loop(0, STEPS, first, 0)
    d = [
        join(line_of(2 * q), line_of(2 * q + 1), strip_of(2 * q), strip_of(2 * q + 1)) for q in range(Q)
    ]
    put_outer(post, spost, collide(d, outer_solid, None))
    to_halo(lambda q, z, j: spost[z, q, pl.ds(j, 1), :], hpost, 1)
    to_halo(
        lambda q, z, j: join(
            strip[0, pl.ds(j * IDX + 40 + 2 * q + z, 1), :], strip[1, pl.ds(j * IDX + 40 + 2 * q + z, 1), :]
        ),
        hcot,
        -1,
    )

    def second(b, carry):
        u = streamed(post, hpost, rows_of(b, 8), 1)
        g = streamed(gpad, hcot, rows_of(b, 8), -1)
        put(gmid, rows_of(b, 8), backward(u, g, solid_at(rows_of(b, 0)), None, True))
        return carry

    lax.fori_loop(0, STEPS, second, 0)
    us = [streamed(post, hpost, [136], 1)] + [
        streamed_strip(lambda q, zs: spost[zs, q], 1, z) for z in range(2)
    ]
    gs = [streamed(gpad, hcot, [136], -1)] + [
        streamed_strip(lambda q, zs: strip_of(40 + 2 * q + zs), -1, z) for z in range(2)
    ]
    u = [join(*[v[q] for v in us]) for q in range(Q)]
    g = [join(*[v[q] for v in gs]) for q in range(Q)]
    put_outer(gmid, smid, backward(u, g, outer_solid, None, False))
    to_halo(lambda q, z, j: smid[z, q, pl.ds(j, 1), :], hmid, -1)

    def third(b, carry):
        g = streamed(gmid, hmid, rows_of(b, 8), -1)
        rows = rows_of(b, 0)
        put(out, rows, backward(block(dist, rows), g, solid_at(rows), hid[b], True))
        return carry

    lax.fori_loop(0, STEPS, third, 0)
    parts[pl.ds(0, 20), :] = acc_in[...].T[:20]
    parts[pl.ds(20, 20), :] = acc_out[pl.ds(0, 20), :]
    flip[...] = jnp.zeros_like(flip)
    for q in range(Q):
        flip[pl.ds(q, 1), :128] = jnp.sum(accb[pl.ds(q * 8, 8), :], axis=0, keepdims=True)
    parts[pl.ds(40, 8), :] = jnp.broadcast_to(jnp.sum(flip[:, :128].T, axis=0, keepdims=True), (8, 128))


def main_call(*args):
    field = pltpu.VMEM((Q, 2, 152, 128), f32)
    halo = pltpu.VMEM((152, 128), f32)
    return pl.pallas_call(
        main_kernel,
        out_shape=[jax.ShapeDtypeStruct((Q, 2, 128, 128), f32), jax.ShapeDtypeStruct((48, 128), f32)],
        in_specs=vmem(len(args)),
        out_specs=vmem(2),
        scratch_shapes=[
            field, field, field,
            pltpu.VMEM((STEPS, 1024, 256 * WIDE), f32),
            halo, halo, halo,
            pltpu.VMEM((2, 640, 128), f32),
            pltpu.VMEM((2, Q, 8, 256), f32),
            pltpu.VMEM((2, Q, 8, 256), f32),
            pltpu.VMEM((128, 256), f32),
            pltpu.VMEM((2 * WIDE, 432, 128), f32),
            pltpu.VMEM((128, 128), f32),
            pltpu.VMEM((32, 128), f32),
            pltpu.VMEM((152, 128), f32),
        ],
        compiler_params=pltpu.CompilerParams(vmem_limit_bytes=58 * 2**20),
    )(*args)


def neighbours(axis):
    size = lax.axis_size(axis)
    up = [(i, (i + 1) % size) for i in range(size)]
    return up, [(j, i) for i, j in up]


def summed(values):
    nx, ny = lax.axis_size("gx"), lax.axis_size("gy")

    def from_partner(values, partner):
        pairs = []
        for x in range(nx):
            for y in range(ny):
                px, py = partner(x, y)
                pairs.append((x * ny + y, px * ny + py))
        return lax.ppermute(values, ("gx", "gy"), pairs)

    if (nx, ny) != (8, 16):
        for k in range(nx.bit_length() - 1):
            values = values + from_partner(values, lambda x, y: (x ^ (1 << k), y))
        for k in range(ny.bit_length() - 1):
            values = values + from_partner(values, lambda x, y: (x, y ^ (1 << k)))
        return values
    got = [values] + [
        from_partner(values, lambda x, y: (x ^ ((d >> 1) & 1), y ^ (d & 1) ^ (((d >> 2) & 1) << 1))) for d in range(1, 8)
    ]
    while len(got) > 1:
        got = [got[i] + got[i + 1] for i in range(0, len(got), 2)]
    copies = jnp.broadcast_to(got[0][None], (4,) + values.shape)
    groups = [[2 * y + low for y in range(4)] for low in range(2)]
    values = lax.all_to_all(copies, "gx", 0, 0, tiled=True, axis_index_groups=groups)
    values = (values[0] + values[1]) + (values[2] + values[3])
    other = (3, 2, 1, 0)
    values = values + from_partner(values, lambda x, y: (x, y ^ 4))
    return values + from_partner(values, lambda x, y: (x, other[y // 4] * 4 + y % 4))


def shards(dist, cot, mask, weight_in, bias_in, weight_out, bias_out):
    send_up, send_down, cols = pack(dist, cot, mask)
    up, down = neighbours("gx")
    from_up = lax.ppermute(send_up, "gx", up)
    from_down = lax.ppermute(send_down, "gx", down)
    nets = make_weights(weight_in, weight_out, bias_in, bias_out)
    cols, nets = lax.optimization_barrier((cols, nets))
    side_up, side_down, edge, lines = corners(from_up, from_down, cols)
    up, down = neighbours("gy")
    from_left = lax.ppermute(side_up, "gy", up)
    from_right = lax.ppermute(side_down, "gy", down)
    grad, parts = main_call(dist, cot, mask, cols, edge, from_left, from_right, lines, *nets)
    total = summed(parts)
    cells = mask.size * lax.axis_size("gx") * lax.axis_size("gy")
    total = total * (1.0 / math.sqrt(cells))
    return grad, total[:19], total[19], total[20:39].T, total[40, :19]


def solution(mesh):
    field = P(None, None, "gx", "gy")
    return jax.shard_map(
        shards,
        mesh=mesh,
        in_specs=(field, field, P(None, "gx", "gy"), P(), P(), P(), P()),
        out_specs=(field, P(), P(), P(), P()),
        check_vma=False,
    )
```

```python
import math

import jax
import jax.numpy as jnp
from jax import lax
from jax.experimental import pallas as pl
from jax.experimental.pallas import tpu as pltpu
from jax.sharding import PartitionSpec as P

VEL = (
    (0, 0, 0), (1, 0, 0), (-1, 0, 0), (0, 1, 0), (0, -1, 0), (0, 0, 1), (0, 0, -1),
    (1, 1, 0), (-1, -1, 0), (1, -1, 0), (-1, 1, 0), (1, 0, 1), (-1, 0, -1), (1, 0, -1),
    (-1, 0, 1), (0, 1, 1), (0, -1, -1), (0, 1, -1), (0, -1, 1),
)
OPP = (0, 2, 1, 4, 3, 6, 5, 8, 7, 10, 9, 12, 11, 14, 13, 16, 15, 18, 17)
Q = 19
WIDE = 8
STEPS = 16 // WIDE
SIDE = tuple(q for q in range(Q) if VEL[q][1])
PLACE = {q: i for i, q in enumerate(SIDE)}
f32 = jnp.float32
bf16 = jnp.bfloat16
NT = (((1,), (1,)), ((), ()))
IDX = 80
COLS = (126, 127, 0, 0, 127, 127, 0, 1)


def iota(shape, dim):
    return lax.broadcasted_iota(jnp.int32, shape, dim)


def vmem(n):
    return [pl.BlockSpec(memory_space=pltpu.VMEM)] * n


def weights_kernel(win, wtout, bias, bias_out, a_in, a_out, b_out, b_in, bias_rows):
    TN = (((0,), (0,)), ((), ()))
    rep = jnp.where(iota((Q, 160), 1) // 8 == iota((Q, 160), 0), 1.0, 0.0).astype(bf16)
    rept = jnp.where(iota((160, Q), 0) // 8 == iota((160, Q), 1), 1.0, 0.0).astype(bf16)
    wide_in = lax.dot_general(win[...], rep, TN, preferred_element_type=f32)
    wide_out = lax.dot_general(wtout[...], rep, TN, preferred_element_type=f32)
    tall_out = jnp.dot(rept, wtout[...], preferred_element_type=f32)
    tall_in = jnp.dot(rept, win[...], preferred_element_type=f32)
    b = jnp.broadcast_to(bias[...], (128, 128)).T
    b = jnp.concatenate([b, b[:, :32]], axis=1)
    high = b.astype(bf16).astype(f32)
    mid = (b - high).astype(bf16).astype(f32)
    low = b - high - mid
    col = iota((128, 160), 1)
    row = iota((160, 128), 0)
    biased = jnp.where(col == 152, high, jnp.where(col == 153, mid, jnp.where(col == 154, low, 0.0)))
    for k in range(8):
        own = (col % 8 == k) & (col < 152)
        own_row = (row % 8 == k) & (row < 152)
        part = slice(k * 128, k * 128 + 128)
        a_in[part, :] = jnp.where(own, wide_in, biased).astype(bf16)
        a_out[part, :] = jnp.where(own, wide_out, 0.0).astype(bf16)
        b_out[:, part] = jnp.where(own_row, tall_out, 0.0).astype(bf16)
        b_in[:, part] = jnp.where(own_row, tall_in, 0.0).astype(bf16)
    for q in range(Q):
        bias_rows[pl.ds(q * 8, 8), :] = jnp.broadcast_to(bias_out[0:1, q : q + 1], (8, 128))


def make_weights(weight_in, weight_out, bias_in, bias_out):
    return pl.pallas_call(
        weights_kernel,
        out_shape=[jax.ShapeDtypeStruct((1024, 160), bf16)] * 2
        + [jax.ShapeDtypeStruct((160, 1024), bf16)] * 2
        + [jax.ShapeDtypeStruct((152, 128), f32)],
        in_specs=vmem(4),
        out_specs=vmem(5),
        cost_estimate=pl.CostEstimate(flops=10**8, bytes_accessed=2 * 10**6, transcendentals=0),
    )(weight_in, weight_out.T, bias_in[None], bias_out[None])


def pack_kernel(dist, cot, mask, up, down, cols, line):
    for out, rows in ((up, (126, 127)), (down, (0, 1))):
        for i, r in enumerate(rows):
            line[pl.ds(0, 38), :] = dist[pl.ds(r, 38, stride=128), :]
            line[pl.ds(38, 2), :] = mask[pl.ds(r, 2, stride=128), :].astype(f32)
            line[pl.ds(40, 38), :] = cot[pl.ds(r, 38, stride=128), :]
            line[pl.ds(78, 2), :] = jnp.zeros((2, 128), f32)
            out[pl.ds(i * 80, 80), :] = line[...].astype(bf16)
    lane, row = iota((8, 128), 1), iota((8, 128), 0)
    pick = jnp.zeros((8, 128), f32)
    for j, y in enumerate(COLS):
        pick = jnp.where((row == j) & (lane == y), 1.0, pick)
    pick = pick.astype(bf16)

    def slabs(ref, first, count, place):
        values = ref[pl.ds(first * 128, count * 128), :].astype(f32).astype(bf16)
        got = lax.dot_general(pick, values, NT, preferred_element_type=f32)
        for i in range(count):
            cols[pl.ds(place + i, 8, stride=IDX), :] = got[:, i * 128 : i * 128 + 128]

    for half in range(2):
        slabs(dist, half * 19, 19, half * 19)
        slabs(cot, half * 19, 19, 40 + half * 19)
    slabs(mask, 0, 2, 38)
    for z in range(2):
        cols[pl.ds(78 + z, 8, stride=IDX), :] = jnp.zeros((8, 128), f32)


def pack(dist, cot, mask):
    return pl.pallas_call(
        pack_kernel,
        out_shape=[jax.ShapeDtypeStruct((160, 128), bf16)] * 2 + [jax.ShapeDtypeStruct((640, 128), f32)],
        in_specs=vmem(3),
        out_specs=vmem(3),
        scratch_shapes=[pltpu.VMEM((80, 128), f32)],
    )(dist.reshape(38 * 128, 128), cot.reshape(38 * 128, 128), mask.reshape(256, 128))


def corner_kernel(from_up, from_down, cols, send_up, send_down, edge, lines):
    sides = ((from_down, 0, 0), (from_down, 1, 1), (from_up, 0, 126), (from_up, 1, 127))
    lane = iota((80, 128), 1)
    got = [ref[pl.ds(i * 80, 80), :].astype(f32) for ref, i, _ in sides]
    for (_, _, place), values in zip(sides, got):
        lines[pl.ds(place % 8, 80, stride=8), :] = values
    for r in range(2, 6):
        lines[pl.ds(r, 80, stride=8), :] = jnp.zeros((80, 128), f32)
    for j, y in enumerate(COLS):
        out = jnp.zeros((80, 128), f32)
        for (_, _, place), values in zip(sides, got):
            out = jnp.where(lane == place, values[:, y : y + 1], out)
        edge[pl.ds(j * 80, 80), :] = out
    for out, first in ((send_up, 0), (send_down, 6)):
        out[:, :128] = cols[pl.ds(first * 80, 160), :].astype(bf16)
        out[:, 128:] = edge[pl.ds(first * 80, 160), :].astype(bf16)


def corners(from_up, from_down, cols):
    return pl.pallas_call(
        corner_kernel,
        out_shape=[jax.ShapeDtypeStruct((160, 256), bf16)] * 2
        + [jax.ShapeDtypeStruct((640, 128), f32)] * 2,
        in_specs=vmem(3),
        out_specs=vmem(4),
    )(from_up, from_down, cols)


def main_kernel(
    dist, cot, mask, cols, edge, from_left, from_right, lines,
    a_in, a_out, b_out, b_in, bias_out,
    out, parts,
    post, gmid, gpad, hid, hpost, hcot, hmid, strip, spost, smid, flip, uo, acc_in, acc_out, accb,
):
    lane = iota((8, 128), 1)
    row8 = iota((8, 128), 0)

    def join(*parts):
        return jnp.concatenate(parts, axis=1)

    strip[0] = cols[...]
    strip[1] = edge[...]
    strip[0, pl.ds(0, 160), :] = from_left[:, :128].astype(f32)
    strip[1, pl.ds(0, 160), :] = from_left[:, 128:].astype(f32)
    strip[0, pl.ds(480, 160), :] = from_right[:, :128].astype(f32)
    strip[1, pl.ds(480, 160), :] = from_right[:, 128:].astype(f32)

    def strip_of(i):
        return join(strip[0, pl.ds(i, 8, stride=IDX), :], strip[1, pl.ds(i, 8, stride=IDX), :])

    def line_of(i):
        return lines[pl.ds(i * 8, 8), :]

    for q in range(Q):
        for z in range(2):
            i = 2 * q + z
            gpad[q, z, pl.ds(8, 128), :] = cot[q, z]
            halo = line_of(40 + i)
            gpad[q, z, pl.ds(0, 8), :] = halo
            gpad[q, z, pl.ds(136, 8), :] = halo
            gpad[q, z, pl.ds(144, 8), :] = cot[q, z, pl.ds(0, 8), :]

    uo[...] = jnp.zeros_like(uo)
    uo[:, pl.ds(19 * 9, 9), :] = jnp.ones((2 * WIDE, 9, 128), f32)
    acc_in[...] = jnp.zeros_like(acc_in)
    acc_out[...] = jnp.zeros_like(acc_out)
    accb[...] = jnp.zeros_like(accb)
    flip[...] = jnp.zeros_like(flip)

    def operand(values):
        ones = jnp.ones(values[0].shape, f32)
        return jnp.concatenate(values + [ones], axis=0).astype(bf16)

    def hidden(values):
        return jnp.tanh(jnp.dot(a_in[...], operand(values), preferred_element_type=f32))

    def collide(d, solid, keep):
        t = hidden(d)
        if keep is not None:
            hid[keep] = t
        o = jnp.dot(b_out[...], t.astype(bf16), preferred_element_type=f32)
        res = []
        for q in range(Q):
            bias = bias_out[pl.ds(q * 8, 8), :]
            val = d[q] + o[q * 8 : q * 8 + 8] + join(*[bias] * (d[q].shape[1] // 128))
            val = jnp.where(solid, d[OPP[q]], val)
            res.append(val.astype(bf16).astype(f32))
        return res

    def backward(u, g, solid, t, partial):
        og = [jnp.where(solid, 0.0, v) for v in g]
        if t is None:
            t = hidden(u)
        hg = jnp.dot(a_out[...], operand(og), preferred_element_type=f32)
        hb = (hg * (1.0 - t * t)).astype(bf16)
        ig = jnp.dot(b_in[...], hb, preferred_element_type=f32)
        if partial:
            act = t.astype(bf16)
            halves = [slice(h * 128, h * 128 + 128) for h in range(2 * WIDE)]
            for q in range(Q):
                for h, part in enumerate(halves):
                    uo[h, pl.ds(q * 9, 8), :] = u[q][:, part]
                    uo[h, pl.ds(216 + q * 9, 8), :] = og[q][:, part]
                accb[pl.ds(q * 8, 8), :] += sum(og[q][:, part] for part in halves)

            def cells(first):
                lines24 = join(
                    *[uo[h, pl.ds(first + k, 24, stride=9), :] for k in range(8) for h in range(2 * WIDE)]
                )
                return jnp.concatenate([lines24, jnp.zeros((8, lines24.shape[1]), f32)], axis=0).astype(bf16)

            def units(values):
                return join(*[values[k * 128 : k * 128 + 128] for k in range(8)])

            left = jnp.concatenate([units(hb), cells(216)], axis=0)
            right = jnp.concatenate([units(act), cells(0)], axis=0)
            both = lax.dot_general(left, right, NT, preferred_element_type=f32)
            acc_in[:, :32] += both[:128, 128:]
            acc_out[...] += both[128:, :128]
        return [
            og[q] + ig[q * 8 : q * 8 + 8] + jnp.where(solid, g[OPP[q]], 0.0) for q in range(Q)
        ]

    def streamed(ref, halo, rows, orient):
        res = []
        for q in range(Q):
            cx, cy, cz = (orient * c for c in VEL[q])
            pieces = []
            for row in rows:
                for z in range(2):
                    zs = (z - cz) % 2
                    v = ref[q, zs, pl.ds(row - cx, 8), :]
                    if cy:
                        k = PLACE[q] * 2 + zs
                        h = halo[pl.ds(row - cx, 8), :][:, k : k + 1]
                        v = pltpu.roll(v, 1 if cy == 1 else 127, 1)
                        v = jnp.where(lane == (0 if cy == 1 else 127), h, v)
                    pieces.append(v)
            res.append(join(*pieces))
        return res

    def streamed_strip(get, orient, z):
        res = []
        for q in range(Q):
            cx, cy, cz = (orient * c for c in VEL[q])
            v = get(q, (z - cz) % 2)
            if cy:
                v = pltpu.roll(v, cy % 8, 0)
            if cx:
                v = pltpu.roll(v, cx % 256, 1)
            res.append(v)
        return res

    def to_halo(get, halo, orient):
        for q in SIDE:
            j = 1 if orient * VEL[q][1] == 1 else 6
            for z in range(2):
                flip[pl.ds(PLACE[q] * 2 + z, 1), :] = get(q, z, j)
        low = flip[:, :128].T
        high = flip[:, 128:].T
        halo[pl.ds(8, 128), :] = low
        outer = jnp.where(row8 < 4, high[0:8], high[120:128])
        halo[pl.ds(136, 8), :] = outer
        halo[pl.ds(0, 8), :] = outer
        halo[pl.ds(144, 8), :] = low[0:8]

    def put(ref, rows, values):
        for q in range(Q):
            for i, row in enumerate(rows):
                for z in range(2):
                    at = i * 256 + z * 128
                    ref[q, z, pl.ds(row, 8), :] = values[q][:, at : at + 128]

    def put_outer(ref, side, values):
        for q in range(Q):
            for z in range(2):
                ref[q, z, pl.ds(136, 8), :] = values[q][:, z * 128 : z * 128 + 128]
                ref[q, z, pl.ds(0, 8), :] = values[q][:, z * 128 : z * 128 + 128]
                ref[q, z, pl.ds(144, 8), :] = ref[q, z, pl.ds(8, 8), :]
                side[z, q] = values[q][:, 256 + z * 256 : 512 + z * 256]

    def block(ref, rows):
        return [join(*[ref[q, z, pl.ds(r, 8), :] for r in rows for z in range(2)]) for q in range(Q)]

    def solid_at(rows):
        return join(*[mask[z, pl.ds(r, 8), :] for r in rows for z in range(2)]) > 0

    outer_solid = join(line_of(38), line_of(39), strip_of(38), strip_of(39)) > 0.5

    def rows_of(b, offset):
        return [pl.multiple_of((b + w * STEPS) * 8, 8) + offset for w in range(WIDE)]

    def first(b, carry):
        put(post, rows_of(b, 8), collide(block(dist, rows_of(b, 0)), solid_at(rows_of(b, 0)), b))
        return carry

    lax.fori_loop(0, STEPS, first, 0)
    d = [
        join(line_of(2 * q), line_of(2 * q + 1), strip_of(2 * q), strip_of(2 * q + 1)) for q in range(Q)
    ]
    put_outer(post, spost, collide(d, outer_solid, None))
    to_halo(lambda q, z, j: spost[z, q, pl.ds(j, 1), :], hpost, 1)
    to_halo(
        lambda q, z, j: join(
            strip[0, pl.ds(j * IDX + 40 + 2 * q + z, 1), :], strip[1, pl.ds(j * IDX + 40 + 2 * q + z, 1), :]
        ),
        hcot,
        -1,
    )

    def second(b, carry):
        u = streamed(post, hpost, rows_of(b, 8), 1)
        g = streamed(gpad, hcot, rows_of(b, 8), -1)
        put(gmid, rows_of(b, 8), backward(u, g, solid_at(rows_of(b, 0)), None, True))
        return carry

    lax.fori_loop(0, STEPS, second, 0)
    us = [streamed(post, hpost, [136], 1)] + [
        streamed_strip(lambda q, zs: spost[zs, q], 1, z) for z in range(2)
    ]
    gs = [streamed(gpad, hcot, [136], -1)] + [
        streamed_strip(lambda q, zs: strip_of(40 + 2 * q + zs), -1, z) for z in range(2)
    ]
    u = [join(*[v[q] for v in us]) for q in range(Q)]
    g = [join(*[v[q] for v in gs]) for q in range(Q)]
    put_outer(gmid, smid, backward(u, g, outer_solid, None, False))
    to_halo(lambda q, z, j: smid[z, q, pl.ds(j, 1), :], hmid, -1)

    def third(b, carry):
        g = streamed(gmid, hmid, rows_of(b, 8), -1)
        rows = rows_of(b, 0)
        put(out, rows, backward(block(dist, rows), g, solid_at(rows), hid[b], True))
        return carry

    lax.fori_loop(0, STEPS, third, 0)
    parts[pl.ds(0, 20), :] = acc_in[...].T[:20]
    parts[pl.ds(20, 20), :] = acc_out[pl.ds(0, 20), :]
    flip[...] = jnp.zeros_like(flip)
    for q in range(Q):
        flip[pl.ds(q, 1), :128] = jnp.sum(accb[pl.ds(q * 8, 8), :], axis=0, keepdims=True)
    parts[pl.ds(40, 8), :] = jnp.broadcast_to(jnp.sum(flip[:, :128].T, axis=0, keepdims=True), (8, 128))


def main_call(*args):
    field = pltpu.VMEM((Q, 2, 152, 128), f32)
    halo = pltpu.VMEM((152, 128), f32)
    return pl.pallas_call(
        main_kernel,
        out_shape=[jax.ShapeDtypeStruct((Q, 2, 128, 128), f32), jax.ShapeDtypeStruct((48, 128), f32)],
        in_specs=vmem(len(args)),
        out_specs=vmem(2),
        scratch_shapes=[
            field, field, field,
            pltpu.VMEM((STEPS, 1024, 256 * WIDE), f32),
            halo, halo, halo,
            pltpu.VMEM((2, 640, 128), f32),
            pltpu.VMEM((2, Q, 8, 256), f32),
            pltpu.VMEM((2, Q, 8, 256), f32),
            pltpu.VMEM((128, 256), f32),
            pltpu.VMEM((2 * WIDE, 432, 128), f32),
            pltpu.VMEM((128, 128), f32),
            pltpu.VMEM((32, 128), f32),
            pltpu.VMEM((152, 128), f32),
        ],
        compiler_params=pltpu.CompilerParams(vmem_limit_bytes=58 * 2**20),
    )(*args)


def neighbours(axis):
    size = lax.axis_size(axis)
    up = [(i, (i + 1) % size) for i in range(size)]
    return up, [(j, i) for i, j in up]


def summed(values):
    nx, ny = lax.axis_size("gx"), lax.axis_size("gy")
    if (nx, ny) == (8, 16):
        stages = (((0, 1), (1, 0), (0, 2)), ((2, 0), (4, 0)), ((0, 4), (0, 8)))
    else:
        stages = [((1 << k, 0),) for k in range(nx.bit_length() - 1)]
        stages += [((0, 1 << k),) for k in range(ny.bit_length() - 1)]
    for bits in stages:
        got = [values]
        for d in range(1, 1 << len(bits)):
            fx = sum(bx for k, (bx, _) in enumerate(bits) if d >> k & 1)
            fy = sum(by for k, (_, by) in enumerate(bits) if d >> k & 1)
            pairs = [(x * ny + y, (x ^ fx) * ny + (y ^ fy)) for x in range(nx) for y in range(ny)]
            got.append(lax.ppermute(values, ("gx", "gy"), pairs))
        while len(got) > 1:
            got = [got[i] + got[i + 1] for i in range(0, len(got), 2)]
        values = got[0]
    return values


def shards(dist, cot, mask, weight_in, bias_in, weight_out, bias_out):
    send_up, send_down, cols = pack(dist, cot, mask)
    up, down = neighbours("gx")
    from_up = lax.ppermute(send_up, "gx", up)
    from_down = lax.ppermute(send_down, "gx", down)
    nets = make_weights(weight_in, weight_out, bias_in, bias_out)
    cols, nets = lax.optimization_barrier((cols, nets))
    side_up, side_down, edge, lines = corners(from_up, from_down, cols)
    up, down = neighbours("gy")
    from_left = lax.ppermute(side_up, "gy", up)
    from_right = lax.ppermute(side_down, "gy", down)
    grad, parts = main_call(dist, cot, mask, cols, edge, from_left, from_right, lines, *nets)
    total = summed(parts)
    cells = mask.size * lax.axis_size("gx") * lax.axis_size("gy")
    total = total * (1.0 / math.sqrt(cells))
    return grad, total[:19], total[19], total[20:39].T, total[40, :19]


def solution(mesh):
    field = P(None, None, "gx", "gy")
    return jax.shard_map(
        shards,
        mesh=mesh,
        in_specs=(field, field, P(None, "gx", "gy"), P(), P(), P(), P()),
        out_specs=(field, P(), P(), P(), P()),
        check_vma=False,
    )
```

```python
import math

import jax
import jax.numpy as jnp
from jax import lax
from jax.experimental import pallas as pl
from jax.experimental.pallas import tpu as pltpu
from jax.sharding import PartitionSpec as P

VEL = (
    (0, 0, 0), (1, 0, 0), (-1, 0, 0), (0, 1, 0), (0, -1, 0), (0, 0, 1), (0, 0, -1),
    (1, 1, 0), (-1, -1, 0), (1, -1, 0), (-1, 1, 0), (1, 0, 1), (-1, 0, -1), (1, 0, -1),
    (-1, 0, 1), (0, 1, 1), (0, -1, -1), (0, 1, -1), (0, -1, 1),
)
OPP = (0, 2, 1, 4, 3, 6, 5, 8, 7, 10, 9, 12, 11, 14, 13, 16, 15, 18, 17)
Q = 19
WIDE = 8
STEPS = 16 // WIDE
SIDE = tuple(q for q in range(Q) if VEL[q][1])
PLACE = {q: i for i, q in enumerate(SIDE)}
f32 = jnp.float32
bf16 = jnp.bfloat16
NT = (((1,), (1,)), ((), ()))
IDX = 80
COLS = (126, 127, 0, 0, 127, 127, 0, 1)


def iota(shape, dim):
    return lax.broadcasted_iota(jnp.int32, shape, dim)


def vmem(n):
    return [pl.BlockSpec(memory_space=pltpu.VMEM)] * n


def weights_kernel(win, wtout, bias, bias_out, a_in, a_out, b_out, b_in, bias_rows):
    TN = (((0,), (0,)), ((), ()))
    rep = jnp.where(iota((Q, 160), 1) // 8 == iota((Q, 160), 0), 1.0, 0.0).astype(bf16)
    rept = jnp.where(iota((160, Q), 0) // 8 == iota((160, Q), 1), 1.0, 0.0).astype(bf16)
    wide_in = lax.dot_general(win[...], rep, TN, preferred_element_type=f32)
    wide_out = lax.dot_general(wtout[...], rep, TN, preferred_element_type=f32)
    tall_out = jnp.dot(rept, wtout[...], preferred_element_type=f32)
    tall_in = jnp.dot(rept, win[...], preferred_element_type=f32)
    b = jnp.broadcast_to(bias[...], (128, 128)).T
    b = jnp.concatenate([b, b[:, :32]], axis=1)
    high = b.astype(bf16).astype(f32)
    mid = (b - high).astype(bf16).astype(f32)
    low = b - high - mid
    col = iota((128, 160), 1)
    row = iota((160, 128), 0)
    biased = jnp.where(col == 152, high, jnp.where(col == 153, mid, jnp.where(col == 154, low, 0.0)))
    for k in range(8):
        own = (col % 8 == k) & (col < 152)
        own_row = (row % 8 == k) & (row < 152)
        part = slice(k * 128, k * 128 + 128)
        a_in[part, :] = jnp.where(own, wide_in, biased).astype(bf16)
        a_out[part, :] = jnp.where(own, wide_out, 0.0).astype(bf16)
        b_out[:, part] = jnp.where(own_row, tall_out, 0.0).astype(bf16)
        b_in[:, part] = jnp.where(own_row, tall_in, 0.0).astype(bf16)
    for q in range(Q):
        bias_rows[pl.ds(q * 8, 8), :] = jnp.broadcast_to(bias_out[0:1, q : q + 1], (8, 128))


def make_weights(weight_in, weight_out, bias_in, bias_out):
    return pl.pallas_call(
        weights_kernel,
        out_shape=[jax.ShapeDtypeStruct((1024, 160), bf16)] * 2
        + [jax.ShapeDtypeStruct((160, 1024), bf16)] * 2
        + [jax.ShapeDtypeStruct((152, 128), f32)],
        in_specs=vmem(4),
        out_specs=vmem(5),
        cost_estimate=pl.CostEstimate(flops=10**8, bytes_accessed=2 * 10**6, transcendentals=0),
    )(weight_in, weight_out.T, bias_in[None], bias_out[None])


def lines_kernel(dist_low, dist_high, cot_low, cot_high, mask_low, mask_high, up, down, line):
    for out, dist, cot, mask, rows in (
        (up, dist_high, cot_high, mask_high, (6, 7)),
        (down, dist_low, cot_low, mask_low, (0, 1)),
    ):
        for i, r in enumerate(rows):
            line[pl.ds(0, 38), :] = dist[:, r, :]
            line[pl.ds(38, 2), :] = mask[:, r, :].astype(f32)
            line[pl.ds(40, 38), :] = cot[:, r, :]
            line[pl.ds(78, 2), :] = jnp.zeros((2, 128), f32)
            out[pl.ds(i * 80, 80), :] = line[...].astype(bf16)


def outer_lines(dist, cot, mask):
    dist, cot = dist.reshape(38, 128, 128), cot.reshape(38, 128, 128)

    def ends(count):
        return [pl.BlockSpec((count, 8, 128), lambda i: (0, 0, 0)), pl.BlockSpec((count, 8, 128), lambda i: (0, 15, 0))]

    return pl.pallas_call(
        lines_kernel,
        grid=(1,),
        out_shape=[jax.ShapeDtypeStruct((160, 128), bf16)] * 2,
        in_specs=ends(38) + ends(38) + ends(2),
        out_specs=[pl.BlockSpec((160, 128), lambda i: (0, 0))] * 2,
        scratch_shapes=[pltpu.VMEM((80, 128), f32)],
    )(dist, dist, cot, cot, mask, mask)


def pack_kernel(dist, cot, mask, cols):
    lane, row = iota((8, 128), 1), iota((8, 128), 0)
    pick = jnp.zeros((8, 128), f32)
    for j, y in enumerate(COLS):
        pick = jnp.where((row == j) & (lane == y), 1.0, pick)
    pick = pick.astype(bf16)

    def slabs(ref, first, count, place):
        values = ref[pl.ds(first * 128, count * 128), :].astype(f32).astype(bf16)
        got = lax.dot_general(pick, values, NT, preferred_element_type=f32)
        for i in range(count):
            cols[pl.ds(place + i, 8, stride=IDX), :] = got[:, i * 128 : i * 128 + 128]

    for half in range(2):
        slabs(dist, half * 19, 19, half * 19)
        slabs(cot, half * 19, 19, 40 + half * 19)
    slabs(mask, 0, 2, 38)
    for z in range(2):
        cols[pl.ds(78 + z, 8, stride=IDX), :] = jnp.zeros((8, 128), f32)


def pack(dist, cot, mask):
    return pl.pallas_call(
        pack_kernel,
        out_shape=jax.ShapeDtypeStruct((640, 128), f32),
        in_specs=vmem(3),
        out_specs=vmem(1)[0],
        cost_estimate=pl.CostEstimate(flops=10**8, bytes_accessed=6 * 10**6, transcendentals=0),
    )(dist.reshape(38 * 128, 128), cot.reshape(38 * 128, 128), mask.reshape(256, 128))


def corner_kernel(from_up, from_down, cols, send_up, send_down, edge, lines):
    sides = ((from_down, 0, 0), (from_down, 1, 1), (from_up, 0, 126), (from_up, 1, 127))
    lane = iota((80, 128), 1)
    got = [ref[pl.ds(i * 80, 80), :].astype(f32) for ref, i, _ in sides]
    for (_, _, place), values in zip(sides, got):
        lines[pl.ds(place % 8, 80, stride=8), :] = values
    for r in range(2, 6):
        lines[pl.ds(r, 80, stride=8), :] = jnp.zeros((80, 128), f32)
    for j, y in enumerate(COLS):
        out = jnp.zeros((80, 128), f32)
        for (_, _, place), values in zip(sides, got):
            out = jnp.where(lane == place, values[:, y : y + 1], out)
        edge[pl.ds(j * 80, 80), :] = out
    for out, first in ((send_up, 0), (send_down, 6)):
        out[:, :128] = cols[pl.ds(first * 80, 160), :].astype(bf16)
        out[:, 128:] = edge[pl.ds(first * 80, 160), :].astype(bf16)


def corners(from_up, from_down, cols):
    return pl.pallas_call(
        corner_kernel,
        out_shape=[jax.ShapeDtypeStruct((160, 256), bf16)] * 2
        + [jax.ShapeDtypeStruct((640, 128), f32)] * 2,
        in_specs=vmem(3),
        out_specs=vmem(4),
    )(from_up, from_down, cols)


def main_kernel(
    dist, cot, mask, cols, edge, from_left, from_right, lines,
    a_in, a_out, b_out, b_in, bias_out,
    out, parts,
    post, gmid, gpad, hid, hpost, hcot, hmid, strip, spost, smid, flip, uo, acc_in, acc_out, accb,
):
    lane = iota((8, 128), 1)
    row8 = iota((8, 128), 0)

    def join(*parts):
        return jnp.concatenate(parts, axis=1)

    strip[0] = cols[...]
    strip[1] = edge[...]
    strip[0, pl.ds(0, 160), :] = from_left[:, :128].astype(f32)
    strip[1, pl.ds(0, 160), :] = from_left[:, 128:].astype(f32)
    strip[0, pl.ds(480, 160), :] = from_right[:, :128].astype(f32)
    strip[1, pl.ds(480, 160), :] = from_right[:, 128:].astype(f32)

    def strip_of(i):
        return join(strip[0, pl.ds(i, 8, stride=IDX), :], strip[1, pl.ds(i, 8, stride=IDX), :])

    def line_of(i):
        return lines[pl.ds(i * 8, 8), :]

    for q in range(Q):
        for z in range(2):
            i = 2 * q + z
            gpad[q, z, pl.ds(8, 128), :] = cot[q, z]
            halo = line_of(40 + i)
            gpad[q, z, pl.ds(0, 8), :] = halo
            gpad[q, z, pl.ds(136, 8), :] = halo
            gpad[q, z, pl.ds(144, 8), :] = cot[q, z, pl.ds(0, 8), :]

    uo[...] = jnp.zeros_like(uo)
    uo[:, pl.ds(19 * 9, 9), :] = jnp.ones((2 * WIDE, 9, 128), f32)
    acc_in[...] = jnp.zeros_like(acc_in)
    acc_out[...] = jnp.zeros_like(acc_out)
    accb[...] = jnp.zeros_like(accb)
    flip[...] = jnp.zeros_like(flip)

    def operand(values):
        ones = jnp.ones(values[0].shape, f32)
        return jnp.concatenate(values + [ones], axis=0).astype(bf16)

    def hidden(values):
        return jnp.tanh(jnp.dot(a_in[...], operand(values), preferred_element_type=f32))

    def collide(d, solid, keep):
        t = hidden(d)
        if keep is not None:
            hid[keep] = t
        o = jnp.dot(b_out[...], t.astype(bf16), preferred_element_type=f32)
        res = []
        for q in range(Q):
            bias = bias_out[pl.ds(q * 8, 8), :]
            val = d[q] + o[q * 8 : q * 8 + 8] + join(*[bias] * (d[q].shape[1] // 128))
            val = jnp.where(solid, d[OPP[q]], val)
            res.append(val.astype(bf16).astype(f32))
        return res

    def backward(u, g, solid, t, partial):
        og = [jnp.where(solid, 0.0, v) for v in g]
        if t is None:
            t = hidden(u)
        hg = jnp.dot(a_out[...], operand(og), preferred_element_type=f32)
        hb = (hg * (1.0 - t * t)).astype(bf16)
        ig = jnp.dot(b_in[...], hb, preferred_element_type=f32)
        if partial:
            act = t.astype(bf16)
            halves = [slice(h * 128, h * 128 + 128) for h in range(2 * WIDE)]
            for q in range(Q):
                for h, part in enumerate(halves):
                    uo[h, pl.ds(q * 9, 8), :] = u[q][:, part]
                    uo[h, pl.ds(216 + q * 9, 8), :] = og[q][:, part]
                accb[pl.ds(q * 8, 8), :] += sum(og[q][:, part] for part in halves)

            def cells(first):
                lines24 = join(
                    *[uo[h, pl.ds(first + k, 24, stride=9), :] for k in range(8) for h in range(2 * WIDE)]
                )
                return jnp.concatenate([lines24, jnp.zeros((8, lines24.shape[1]), f32)], axis=0).astype(bf16)

            def units(values):
                return join(*[values[k * 128 : k * 128 + 128] for k in range(8)])

            left = jnp.concatenate([units(hb), cells(216)], axis=0)
            right = jnp.concatenate([units(act), cells(0)], axis=0)
            both = lax.dot_general(left, right, NT, preferred_element_type=f32)
            acc_in[:, :32] += both[:128, 128:]
            acc_out[...] += both[128:, :128]
        return [
            og[q] + ig[q * 8 : q * 8 + 8] + jnp.where(solid, g[OPP[q]], 0.0) for q in range(Q)
        ]

    def streamed(ref, halo, rows, orient):
        res = []
        for q in range(Q):
            cx, cy, cz = (orient * c for c in VEL[q])
            pieces = []
            for row in rows:
                for z in range(2):
                    zs = (z - cz) % 2
                    v = ref[q, zs, pl.ds(row - cx, 8), :]
                    if cy:
                        k = PLACE[q] * 2 + zs
                        h = halo[pl.ds(row - cx, 8), :][:, k : k + 1]
                        v = pltpu.roll(v, 1 if cy == 1 else 127, 1)
                        v = jnp.where(lane == (0 if cy == 1 else 127), h, v)
                    pieces.append(v)
            res.append(join(*pieces))
        return res

    def streamed_strip(get, orient, z):
        res = []
        for q in range(Q):
            cx, cy, cz = (orient * c for c in VEL[q])
            v = get(q, (z - cz) % 2)
            if cy:
                v = pltpu.roll(v, cy % 8, 0)
            if cx:
                v = pltpu.roll(v, cx % 256, 1)
            res.append(v)
        return res

    def to_halo(get, halo, orient):
        for q in SIDE:
            j = 1 if orient * VEL[q][1] == 1 else 6
            for z in range(2):
                flip[pl.ds(PLACE[q] * 2 + z, 1), :] = get(q, z, j)
        low = flip[:, :128].T
        high = flip[:, 128:].T
        halo[pl.ds(8, 128), :] = low
        outer = jnp.where(row8 < 4, high[0:8], high[120:128])
        halo[pl.ds(136, 8), :] = outer
        halo[pl.ds(0, 8), :] = outer
        halo[pl.ds(144, 8), :] = low[0:8]

    def put(ref, rows, values):
        for q in range(Q):
            for i, row in enumerate(rows):
                for z in range(2):
                    at = i * 256 + z * 128
                    ref[q, z, pl.ds(row, 8), :] = values[q][:, at : at + 128]

    def put_outer(ref, side, values):
        for q in range(Q):
            for z in range(2):
                ref[q, z, pl.ds(136, 8), :] = values[q][:, z * 128 : z * 128 + 128]
                ref[q, z, pl.ds(0, 8), :] = values[q][:, z * 128 : z * 128 + 128]
                ref[q, z, pl.ds(144, 8), :] = ref[q, z, pl.ds(8, 8), :]
                side[z, q] = values[q][:, 256 + z * 256 : 512 + z * 256]

    def block(ref, rows):
        return [join(*[ref[q, z, pl.ds(r, 8), :] for r in rows for z in range(2)]) for q in range(Q)]

    def solid_at(rows):
        return join(*[mask[z, pl.ds(r, 8), :] for r in rows for z in range(2)]) > 0

    outer_solid = join(line_of(38), line_of(39), strip_of(38), strip_of(39)) > 0.5

    def rows_of(b, offset):
        return [pl.multiple_of((b + w * STEPS) * 8, 8) + offset for w in range(WIDE)]

    def first(b, carry):
        put(post, rows_of(b, 8), collide(block(dist, rows_of(b, 0)), solid_at(rows_of(b, 0)), b))
        return carry

    lax.fori_loop(0, STEPS, first, 0)
    d = [
        join(line_of(2 * q), line_of(2 * q + 1), strip_of(2 * q), strip_of(2 * q + 1)) for q in range(Q)
    ]
    put_outer(post, spost, collide(d, outer_solid, None))
    to_halo(lambda q, z, j: spost[z, q, pl.ds(j, 1), :], hpost, 1)
    to_halo(
        lambda q, z, j: join(
            strip[0, pl.ds(j * IDX + 40 + 2 * q + z, 1), :], strip[1, pl.ds(j * IDX + 40 + 2 * q + z, 1), :]
        ),
        hcot,
        -1,
    )

    def second(b, carry):
        u = streamed(post, hpost, rows_of(b, 8), 1)
        g = streamed(gpad, hcot, rows_of(b, 8), -1)
        put(gmid, rows_of(b, 8), backward(u, g, solid_at(rows_of(b, 0)), None, True))
        return carry

    lax.fori_loop(0, STEPS, second, 0)
    us = [streamed(post, hpost, [136], 1)] + [
        streamed_strip(lambda q, zs: spost[zs, q], 1, z) for z in range(2)
    ]
    gs = [streamed(gpad, hcot, [136], -1)] + [
        streamed_strip(lambda q, zs: strip_of(40 + 2 * q + zs), -1, z) for z in range(2)
    ]
    u = [join(*[v[q] for v in us]) for q in range(Q)]
    g = [join(*[v[q] for v in gs]) for q in range(Q)]
    put_outer(gmid, smid, backward(u, g, outer_solid, None, False))
    to_halo(lambda q, z, j: smid[z, q, pl.ds(j, 1), :], hmid, -1)

    def third(b, carry):
        g = streamed(gmid, hmid, rows_of(b, 8), -1)
        rows = rows_of(b, 0)
        put(out, rows, backward(block(dist, rows), g, solid_at(rows), hid[b], True))
        return carry

    lax.fori_loop(0, STEPS, third, 0)
    parts[pl.ds(0, 20), :] = acc_in[...].T[:20]
    parts[pl.ds(20, 20), :] = acc_out[pl.ds(0, 20), :]
    flip[...] = jnp.zeros_like(flip)
    for q in range(Q):
        flip[pl.ds(q, 1), :128] = jnp.sum(accb[pl.ds(q * 8, 8), :], axis=0, keepdims=True)
    parts[pl.ds(40, 8), :] = jnp.broadcast_to(jnp.sum(flip[:, :128].T, axis=0, keepdims=True), (8, 128))


def main_call(*args):
    field = pltpu.VMEM((Q, 2, 152, 128), f32)
    halo = pltpu.VMEM((152, 128), f32)
    return pl.pallas_call(
        main_kernel,
        out_shape=[jax.ShapeDtypeStruct((Q, 2, 128, 128), f32), jax.ShapeDtypeStruct((48, 128), f32)],
        in_specs=vmem(len(args)),
        out_specs=vmem(2),
        scratch_shapes=[
            field, field, field,
            pltpu.VMEM((STEPS, 1024, 256 * WIDE), f32),
            halo, halo, halo,
            pltpu.VMEM((2, 640, 128), f32),
            pltpu.VMEM((2, Q, 8, 256), f32),
            pltpu.VMEM((2, Q, 8, 256), f32),
            pltpu.VMEM((128, 256), f32),
            pltpu.VMEM((2 * WIDE, 432, 128), f32),
            pltpu.VMEM((128, 128), f32),
            pltpu.VMEM((32, 128), f32),
            pltpu.VMEM((152, 128), f32),
        ],
        compiler_params=pltpu.CompilerParams(vmem_limit_bytes=58 * 2**20),
    )(*args)


def neighbours(axis):
    size = lax.axis_size(axis)
    up = [(i, (i + 1) % size) for i in range(size)]
    return up, [(j, i) for i, j in up]


def summed(values):
    nx, ny = lax.axis_size("gx"), lax.axis_size("gy")
    if (nx, ny) == (8, 16):
        stages = (((0, 1), (1, 0), (0, 2)), ((2, 0), (4, 0)), ((0, 4), (0, 8)))
    else:
        stages = [((1 << k, 0),) for k in range(nx.bit_length() - 1)]
        stages += [((0, 1 << k),) for k in range(ny.bit_length() - 1)]
    for bits in stages:
        got = [values]
        for d in range(1, 1 << len(bits)):
            fx = sum(bx for k, (bx, _) in enumerate(bits) if d >> k & 1)
            fy = sum(by for k, (_, by) in enumerate(bits) if d >> k & 1)
            pairs = [(x * ny + y, (x ^ fx) * ny + (y ^ fy)) for x in range(nx) for y in range(ny)]
            got.append(lax.ppermute(values, ("gx", "gy"), pairs))
        while len(got) > 1:
            got = [got[i] + got[i + 1] for i in range(0, len(got), 2)]
        values = got[0]
    return values


def shards(dist, cot, mask, weight_in, bias_in, weight_out, bias_out):
    send_up, send_down = outer_lines(dist, cot, mask)
    up, down = neighbours("gx")
    from_up = lax.ppermute(send_up, "gx", up)
    from_down = lax.ppermute(send_down, "gx", down)
    cols = pack(dist, cot, mask)
    side_up, side_down, edge, lines = corners(from_up, from_down, cols)
    up, down = neighbours("gy")
    from_left = lax.ppermute(side_up, "gy", up)
    from_right = lax.ppermute(side_down, "gy", down)
    weight_in, _ = lax.optimization_barrier((weight_in, edge))
    nets = make_weights(weight_in, weight_out, bias_in, bias_out)
    grad, parts = main_call(dist, cot, mask, cols, edge, from_left, from_right, lines, *nets)
    total = summed(parts)
    cells = mask.size * lax.axis_size("gx") * lax.axis_size("gy")
    total = total * (1.0 / math.sqrt(cells))
    return grad, total[:19], total[19], total[20:39].T, total[40, :19]


def solution(mesh):
    field = P(None, None, "gx", "gy")
    return jax.shard_map(
        shards,
        mesh=mesh,
        in_specs=(field, field, P(None, "gx", "gy"), P(), P(), P(), P()),
        out_specs=(field, P(), P(), P(), P()),
        check_vma=False,
    )
```

```python
import math

import jax
import jax.numpy as jnp
from jax import lax
from jax.experimental import pallas as pl
from jax.experimental.pallas import tpu as pltpu
from jax.sharding import PartitionSpec as P

VEL = (
    (0, 0, 0), (1, 0, 0), (-1, 0, 0), (0, 1, 0), (0, -1, 0), (0, 0, 1), (0, 0, -1),
    (1, 1, 0), (-1, -1, 0), (1, -1, 0), (-1, 1, 0), (1, 0, 1), (-1, 0, -1), (1, 0, -1),
    (-1, 0, 1), (0, 1, 1), (0, -1, -1), (0, 1, -1), (0, -1, 1),
)
OPP = (0, 2, 1, 4, 3, 6, 5, 8, 7, 10, 9, 12, 11, 14, 13, 16, 15, 18, 17)
Q = 19
WIDE = 8
STEPS = 16 // WIDE
SIDE = tuple(q for q in range(Q) if VEL[q][1])
PLACE = {q: i for i, q in enumerate(SIDE)}
f32 = jnp.float32
bf16 = jnp.bfloat16
NT = (((1,), (1,)), ((), ()))
IDX = 80
COLS = (126, 127, 0, 0, 127, 127, 0, 1)


def iota(shape, dim):
    return lax.broadcasted_iota(jnp.int32, shape, dim)


def vmem(n):
    return [pl.BlockSpec(memory_space=pltpu.VMEM)] * n


def weights_kernel(win, wtout, bias, bias_out, a_in, a_out, b_out, b_in, bias_rows):
    TN = (((0,), (0,)), ((), ()))
    rep = jnp.where(iota((Q, 160), 1) // 8 == iota((Q, 160), 0), 1.0, 0.0).astype(bf16)
    rept = jnp.where(iota((160, Q), 0) // 8 == iota((160, Q), 1), 1.0, 0.0).astype(bf16)
    wide_in = lax.dot_general(win[...], rep, TN, preferred_element_type=f32)
    wide_out = lax.dot_general(wtout[...], rep, TN, preferred_element_type=f32)
    tall_out = jnp.dot(rept, wtout[...], preferred_element_type=f32)
    tall_in = jnp.dot(rept, win[...], preferred_element_type=f32)
    b = jnp.broadcast_to(bias[...], (128, 128)).T
    b = jnp.concatenate([b, b[:, :32]], axis=1)
    high = b.astype(bf16).astype(f32)
    mid = (b - high).astype(bf16).astype(f32)
    low = b - high - mid
    col = iota((128, 160), 1)
    row = iota((160, 128), 0)
    biased = jnp.where(col == 152, high, jnp.where(col == 153, mid, jnp.where(col == 154, low, 0.0)))
    for k in range(8):
        own = (col % 8 == k) & (col < 152)
        own_row = (row % 8 == k) & (row < 152)
        part = slice(k * 128, k * 128 + 128)
        a_in[part, :] = jnp.where(own, wide_in, biased).astype(bf16)
        a_out[part, :] = jnp.where(own, wide_out, 0.0).astype(bf16)
        b_out[:, part] = jnp.where(own_row, tall_out, 0.0).astype(bf16)
        b_in[:, part] = jnp.where(own_row, tall_in, 0.0).astype(bf16)
    for q in range(Q):
        bias_rows[pl.ds(q * 8, 8), :] = jnp.broadcast_to(bias_out[0:1, q : q + 1], (8, 128))


def make_weights(weight_in, weight_out, bias_in, bias_out):
    return pl.pallas_call(
        weights_kernel,
        out_shape=[jax.ShapeDtypeStruct((1024, 160), bf16)] * 2
        + [jax.ShapeDtypeStruct((160, 1024), bf16)] * 2
        + [jax.ShapeDtypeStruct((152, 128), f32)],
        in_specs=vmem(4),
        out_specs=vmem(5),
        cost_estimate=pl.CostEstimate(flops=10**8, bytes_accessed=2 * 10**6, transcendentals=0),
    )(weight_in, weight_out.T, bias_in[None], bias_out[None])


def lines_kernel(dist_low, dist_high, cot_low, cot_high, mask_low, mask_high, up, down, line):
    for out, dist, cot, mask, rows in (
        (up, dist_high, cot_high, mask_high, (6, 7)),
        (down, dist_low, cot_low, mask_low, (0, 1)),
    ):
        for i, r in enumerate(rows):
            line[pl.ds(0, 38), :] = dist[:, r, :]
            line[pl.ds(38, 2), :] = mask[:, r, :].astype(f32)
            line[pl.ds(40, 38), :] = cot[:, r, :]
            line[pl.ds(78, 2), :] = jnp.zeros((2, 128), f32)
            out[pl.ds(i * 80, 80), :] = line[...].astype(bf16)


def outer_lines(dist, cot, mask):
    dist, cot = dist.reshape(38, 128, 128), cot.reshape(38, 128, 128)

    def ends(count):
        return [pl.BlockSpec((count, 8, 128), lambda i: (0, 0, 0)), pl.BlockSpec((count, 8, 128), lambda i: (0, 15, 0))]

    return pl.pallas_call(
        lines_kernel,
        grid=(1,),
        out_shape=[jax.ShapeDtypeStruct((160, 128), bf16)] * 2,
        in_specs=ends(38) + ends(38) + ends(2),
        out_specs=[pl.BlockSpec((160, 128), lambda i: (0, 0))] * 2,
        scratch_shapes=[pltpu.VMEM((80, 128), f32)],
    )(dist, dist, cot, cot, mask, mask)


def pack_kernel(dist, cot, mask, cols):
    lane, row = iota((8, 128), 1), iota((8, 128), 0)
    pick = jnp.zeros((8, 128), f32)
    for j, y in enumerate(COLS):
        pick = jnp.where((row == j) & (lane == y), 1.0, pick)
    pick = pick.astype(bf16)

    def slabs(ref, first, count, place):
        values = ref[pl.ds(first * 128, count * 128), :].astype(f32).astype(bf16)
        got = lax.dot_general(pick, values, NT, preferred_element_type=f32)
        for i in range(count):
            cols[pl.ds(place + i, 8, stride=IDX), :] = got[:, i * 128 : i * 128 + 128]

    for half in range(2):
        slabs(dist, half * 19, 19, half * 19)
        slabs(cot, half * 19, 19, 40 + half * 19)
    slabs(mask, 0, 2, 38)
    for z in range(2):
        cols[pl.ds(78 + z, 8, stride=IDX), :] = jnp.zeros((8, 128), f32)


def pack(dist, cot, mask):
    return pl.pallas_call(
        pack_kernel,
        out_shape=jax.ShapeDtypeStruct((640, 128), f32),
        in_specs=vmem(3),
        out_specs=vmem(1)[0],
        cost_estimate=pl.CostEstimate(flops=10**8, bytes_accessed=6 * 10**6, transcendentals=0),
    )(dist.reshape(38 * 128, 128), cot.reshape(38 * 128, 128), mask.reshape(256, 128))


def corner_kernel(received, cols, send_up, send_down, edge, lines):
    sides = ((2, 0), (3, 1), (0, 126), (1, 127))
    lane = iota((80, 128), 1)
    got = [received[pl.ds(i * 80, 80), :].astype(f32) for i, _ in sides]
    for (_, place), values in zip(sides, got):
        lines[pl.ds(place % 8, 80, stride=8), :] = values
    for r in range(2, 6):
        lines[pl.ds(r, 80, stride=8), :] = jnp.zeros((80, 128), f32)
    for j, y in enumerate(COLS):
        out = jnp.zeros((80, 128), f32)
        for (_, place), values in zip(sides, got):
            out = jnp.where(lane == place, values[:, y : y + 1], out)
        edge[pl.ds(j * 80, 80), :] = out
    for out, first in ((send_up, 0), (send_down, 6)):
        out[:, :128] = cols[pl.ds(first * 80, 160), :].astype(bf16)
        out[:, 128:] = edge[pl.ds(first * 80, 160), :].astype(bf16)


def corners(received, cols):
    return pl.pallas_call(
        corner_kernel,
        out_shape=[jax.ShapeDtypeStruct((160, 256), bf16)] * 2
        + [jax.ShapeDtypeStruct((640, 128), f32)] * 2,
        in_specs=vmem(2),
        out_specs=vmem(4),
    )(received, cols)


def main_kernel(
    dist, cot, mask, cols, edge, from_left, from_right, lines,
    a_in, a_out, b_out, b_in, bias_out,
    out, parts,
    post, gmid, gpad, hid, hpost, hcot, hmid, strip, spost, smid, flip, uo, acc_in, acc_out, accb,
):
    lane = iota((8, 128), 1)
    row8 = iota((8, 128), 0)

    def join(*parts):
        return jnp.concatenate(parts, axis=1)

    strip[0] = cols[...]
    strip[1] = edge[...]
    strip[0, pl.ds(0, 160), :] = from_left[:, :128].astype(f32)
    strip[1, pl.ds(0, 160), :] = from_left[:, 128:].astype(f32)
    strip[0, pl.ds(480, 160), :] = from_right[:, :128].astype(f32)
    strip[1, pl.ds(480, 160), :] = from_right[:, 128:].astype(f32)

    def strip_of(i):
        return join(strip[0, pl.ds(i, 8, stride=IDX), :], strip[1, pl.ds(i, 8, stride=IDX), :])

    def line_of(i):
        return lines[pl.ds(i * 8, 8), :]

    for q in range(Q):
        for z in range(2):
            i = 2 * q + z
            gpad[q, z, pl.ds(8, 128), :] = cot[q, z]
            halo = line_of(40 + i)
            gpad[q, z, pl.ds(0, 8), :] = halo
            gpad[q, z, pl.ds(136, 8), :] = halo
            gpad[q, z, pl.ds(144, 8), :] = cot[q, z, pl.ds(0, 8), :]

    uo[...] = jnp.zeros_like(uo)
    uo[:, pl.ds(19 * 9, 9), :] = jnp.ones((2 * WIDE, 9, 128), f32)
    acc_in[...] = jnp.zeros_like(acc_in)
    acc_out[...] = jnp.zeros_like(acc_out)
    accb[...] = jnp.zeros_like(accb)
    flip[...] = jnp.zeros_like(flip)

    def operand(values):
        ones = jnp.ones(values[0].shape, f32)
        return jnp.concatenate(values + [ones], axis=0).astype(bf16)

    def hidden(values):
        return jnp.tanh(jnp.dot(a_in[...], operand(values), preferred_element_type=f32))

    def collide(d, solid, keep):
        t = hidden(d)
        if keep is not None:
            hid[keep] = t
        o = jnp.dot(b_out[...], t.astype(bf16), preferred_element_type=f32)
        res = []
        for q in range(Q):
            bias = bias_out[pl.ds(q * 8, 8), :]
            val = d[q] + o[q * 8 : q * 8 + 8] + join(*[bias] * (d[q].shape[1] // 128))
            val = jnp.where(solid, d[OPP[q]], val)
            res.append(val.astype(bf16).astype(f32))
        return res

    def backward(u, g, solid, t, partial):
        og = [jnp.where(solid, 0.0, v) for v in g]
        if t is None:
            t = hidden(u)
        hg = jnp.dot(a_out[...], operand(og), preferred_element_type=f32)
        hb = (hg * (1.0 - t * t)).astype(bf16)
        ig = jnp.dot(b_in[...], hb, preferred_element_type=f32)
        if partial:
            act = t.astype(bf16)
            halves = [slice(h * 128, h * 128 + 128) for h in range(2 * WIDE)]
            for q in range(Q):
                for h, part in enumerate(halves):
                    uo[h, pl.ds(q * 9, 8), :] = u[q][:, part]
                    uo[h, pl.ds(216 + q * 9, 8), :] = og[q][:, part]
                accb[pl.ds(q * 8, 8), :] += sum(og[q][:, part] for part in halves)

            def cells(first):
                lines24 = join(
                    *[uo[h, pl.ds(first + k, 24, stride=9), :] for k in range(8) for h in range(2 * WIDE)]
                )
                return jnp.concatenate([lines24, jnp.zeros((8, lines24.shape[1]), f32)], axis=0).astype(bf16)

            def units(values):
                return join(*[values[k * 128 : k * 128 + 128] for k in range(8)])

            left = jnp.concatenate([units(hb), cells(216)], axis=0)
            right = jnp.concatenate([units(act), cells(0)], axis=0)
            both = lax.dot_general(left, right, NT, preferred_element_type=f32)
            acc_in[:, :32] += both[:128, 128:]
            acc_out[...] += both[128:, :128]
        return [
            og[q] + ig[q * 8 : q * 8 + 8] + jnp.where(solid, g[OPP[q]], 0.0) for q in range(Q)
        ]

    def streamed(ref, halo, rows, orient):
        res = []
        for q in range(Q):
            cx, cy, cz = (orient * c for c in VEL[q])
            pieces = []
            for row in rows:
                for z in range(2):
                    zs = (z - cz) % 2
                    v = ref[q, zs, pl.ds(row - cx, 8), :]
                    if cy:
                        k = PLACE[q] * 2 + zs
                        h = halo[pl.ds(row - cx, 8), :][:, k : k + 1]
                        v = pltpu.roll(v, 1 if cy == 1 else 127, 1)
                        v = jnp.where(lane == (0 if cy == 1 else 127), h, v)
                    pieces.append(v)
            res.append(join(*pieces))
        return res

    def streamed_strip(get, orient, z):
        res = []
        for q in range(Q):
            cx, cy, cz = (orient * c for c in VEL[q])
            v = get(q, (z - cz) % 2)
            if cy:
                v = pltpu.roll(v, cy % 8, 0)
            if cx:
                v = pltpu.roll(v, cx % 256, 1)
            res.append(v)
        return res

    def to_halo(get, halo, orient):
        for q in SIDE:
            j = 1 if orient * VEL[q][1] == 1 else 6
            for z in range(2):
                flip[pl.ds(PLACE[q] * 2 + z, 1), :] = get(q, z, j)
        low = flip[:, :128].T
        high = flip[:, 128:].T
        halo[pl.ds(8, 128), :] = low
        outer = jnp.where(row8 < 4, high[0:8], high[120:128])
        halo[pl.ds(136, 8), :] = outer
        halo[pl.ds(0, 8), :] = outer
        halo[pl.ds(144, 8), :] = low[0:8]

    def put(ref, rows, values):
        for q in range(Q):
            for i, row in enumerate(rows):
                for z in range(2):
                    at = i * 256 + z * 128
                    ref[q, z, pl.ds(row, 8), :] = values[q][:, at : at + 128]

    def put_outer(ref, side, values):
        for q in range(Q):
            for z in range(2):
                ref[q, z, pl.ds(136, 8), :] = values[q][:, z * 128 : z * 128 + 128]
                ref[q, z, pl.ds(0, 8), :] = values[q][:, z * 128 : z * 128 + 128]
                ref[q, z, pl.ds(144, 8), :] = ref[q, z, pl.ds(8, 8), :]
                side[z, q] = values[q][:, 256 + z * 256 : 512 + z * 256]

    def block(ref, rows):
        return [join(*[ref[q, z, pl.ds(r, 8), :] for r in rows for z in range(2)]) for q in range(Q)]

    def solid_at(rows):
        return join(*[mask[z, pl.ds(r, 8), :] for r in rows for z in range(2)]) > 0

    outer_solid = join(line_of(38), line_of(39), strip_of(38), strip_of(39)) > 0.5

    def rows_of(b, offset):
        return [pl.multiple_of((b + w * STEPS) * 8, 8) + offset for w in range(WIDE)]

    def first(b, carry):
        put(post, rows_of(b, 8), collide(block(dist, rows_of(b, 0)), solid_at(rows_of(b, 0)), b))
        return carry

    lax.fori_loop(0, STEPS, first, 0)
    d = [
        join(line_of(2 * q), line_of(2 * q + 1), strip_of(2 * q), strip_of(2 * q + 1)) for q in range(Q)
    ]
    put_outer(post, spost, collide(d, outer_solid, None))
    to_halo(lambda q, z, j: spost[z, q, pl.ds(j, 1), :], hpost, 1)
    to_halo(
        lambda q, z, j: join(
            strip[0, pl.ds(j * IDX + 40 + 2 * q + z, 1), :], strip[1, pl.ds(j * IDX + 40 + 2 * q + z, 1), :]
        ),
        hcot,
        -1,
    )

    def second(b, carry):
        u = streamed(post, hpost, rows_of(b, 8), 1)
        g = streamed(gpad, hcot, rows_of(b, 8), -1)
        put(gmid, rows_of(b, 8), backward(u, g, solid_at(rows_of(b, 0)), None, True))
        return carry

    lax.fori_loop(0, STEPS, second, 0)
    us = [streamed(post, hpost, [136], 1)] + [
        streamed_strip(lambda q, zs: spost[zs, q], 1, z) for z in range(2)
    ]
    gs = [streamed(gpad, hcot, [136], -1)] + [
        streamed_strip(lambda q, zs: strip_of(40 + 2 * q + zs), -1, z) for z in range(2)
    ]
    u = [join(*[v[q] for v in us]) for q in range(Q)]
    g = [join(*[v[q] for v in gs]) for q in range(Q)]
    put_outer(gmid, smid, backward(u, g, outer_solid, None, False))
    to_halo(lambda q, z, j: smid[z, q, pl.ds(j, 1), :], hmid, -1)

    def third(b, carry):
        g = streamed(gmid, hmid, rows_of(b, 8), -1)
        rows = rows_of(b, 0)
        put(out, rows, backward(block(dist, rows), g, solid_at(rows), hid[b], True))
        return carry

    lax.fori_loop(0, STEPS, third, 0)
    parts[pl.ds(0, 20), :] = acc_in[...].T[:20]
    parts[pl.ds(20, 20), :] = acc_out[pl.ds(0, 20), :]
    flip[...] = jnp.zeros_like(flip)
    for q in range(Q):
        flip[pl.ds(q, 1), :128] = jnp.sum(accb[pl.ds(q * 8, 8), :], axis=0, keepdims=True)
    parts[pl.ds(40, 8), :] = jnp.broadcast_to(jnp.sum(flip[:, :128].T, axis=0, keepdims=True), (8, 128))


def main_call(*args):
    field = pltpu.VMEM((Q, 2, 152, 128), f32)
    halo = pltpu.VMEM((152, 128), f32)
    return pl.pallas_call(
        main_kernel,
        out_shape=[jax.ShapeDtypeStruct((Q, 2, 128, 128), f32), jax.ShapeDtypeStruct((48, 128), f32)],
        in_specs=vmem(len(args)),
        out_specs=vmem(2),
        scratch_shapes=[
            field, field, field,
            pltpu.VMEM((STEPS, 1024, 256 * WIDE), f32),
            halo, halo, halo,
            pltpu.VMEM((2, 640, 128), f32),
            pltpu.VMEM((2, Q, 8, 256), f32),
            pltpu.VMEM((2, Q, 8, 256), f32),
            pltpu.VMEM((128, 256), f32),
            pltpu.VMEM((2 * WIDE, 432, 128), f32),
            pltpu.VMEM((128, 128), f32),
            pltpu.VMEM((32, 128), f32),
            pltpu.VMEM((152, 128), f32),
        ],
        compiler_params=pltpu.CompilerParams(vmem_limit_bytes=58 * 2**20),
    )(*args)


def neighbours(axis):
    size = lax.axis_size(axis)
    up = [(i, (i + 1) % size) for i in range(size)]
    return up, [(j, i) for i, j in up]


def summed(values):
    nx, ny = lax.axis_size("gx"), lax.axis_size("gy")
    if (nx, ny) == (8, 16):
        stages = (((0, 1), (1, 0), (0, 2)), ((2, 0), (4, 0)), ((0, 4), (0, 8)))
    else:
        stages = [((1 << k, 0),) for k in range(nx.bit_length() - 1)]
        stages += [((0, 1 << k),) for k in range(ny.bit_length() - 1)]
    for bits in stages:
        got = [values]
        for d in range(1, 1 << len(bits)):
            fx = sum(bx for k, (bx, _) in enumerate(bits) if d >> k & 1)
            fy = sum(by for k, (_, by) in enumerate(bits) if d >> k & 1)
            pairs = [(x * ny + y, (x ^ fx) * ny + (y ^ fy)) for x in range(nx) for y in range(ny)]
            got.append(lax.ppermute(values, ("gx", "gy"), pairs))
        while len(got) > 1:
            got = [got[i] + got[i + 1] for i in range(0, len(got), 2)]
        values = got[0]
    return values


def shards(dist, cot, mask, weight_in, bias_in, weight_out, bias_out):
    send_up, send_down = outer_lines(dist, cot, mask)
    up, down = neighbours("gx")
    from_up = lax.ppermute(send_up, "gx", up)
    from_down = lax.ppermute(send_down, "gx", down)
    cols = pack(dist, cot, mask)
    side_up, side_down, edge, lines = corners(jnp.concatenate([from_up, from_down]), cols)
    up, down = neighbours("gy")
    from_left = lax.ppermute(side_up, "gy", up)
    from_right = lax.ppermute(side_down, "gy", down)
    weight_in, _ = lax.optimization_barrier((weight_in, edge))
    nets = make_weights(weight_in, weight_out, bias_in, bias_out)
    grad, parts = main_call(dist, cot, mask, cols, edge, from_left, from_right, lines, *nets)
    total = summed(parts)
    cells = mask.size * lax.axis_size("gx") * lax.axis_size("gy")
    total = total * (1.0 / math.sqrt(cells))
    return grad, total[:19], total[19], total[20:39].T, total[40, :19]


def solution(mesh):
    field = P(None, None, "gx", "gy")
    return jax.shard_map(
        shards,
        mesh=mesh,
        in_specs=(field, field, P(None, "gx", "gy"), P(), P(), P(), P()),
        out_specs=(field, P(), P(), P(), P()),
        check_vma=False,
    )
```

```python
import math

import jax
import jax.numpy as jnp
from jax import lax
from jax.experimental import pallas as pl
from jax.experimental.pallas import tpu as pltpu
from jax.sharding import PartitionSpec as P

VEL = (
    (0, 0, 0), (1, 0, 0), (-1, 0, 0), (0, 1, 0), (0, -1, 0), (0, 0, 1), (0, 0, -1),
    (1, 1, 0), (-1, -1, 0), (1, -1, 0), (-1, 1, 0), (1, 0, 1), (-1, 0, -1), (1, 0, -1),
    (-1, 0, 1), (0, 1, 1), (0, -1, -1), (0, 1, -1), (0, -1, 1),
)
OPP = (0, 2, 1, 4, 3, 6, 5, 8, 7, 10, 9, 12, 11, 14, 13, 16, 15, 18, 17)
Q = 19
WIDE = 8
STEPS = 16 // WIDE
SIDE = tuple(q for q in range(Q) if VEL[q][1])
PLACE = {q: i for i, q in enumerate(SIDE)}
f32 = jnp.float32
bf16 = jnp.bfloat16
NT = (((1,), (1,)), ((), ()))
IDX = 80
COLS = (126, 127, 0, 0, 127, 127, 0, 1)


def iota(shape, dim):
    return lax.broadcasted_iota(jnp.int32, shape, dim)


def vmem(n):
    return [pl.BlockSpec(memory_space=pltpu.VMEM)] * n


def weights_kernel(win, wtout, bias, bias_out, a_in, a_out, b_out, b_in, bias_rows):
    TN = (((0,), (0,)), ((), ()))
    rep = jnp.where(iota((Q, 160), 1) // 8 == iota((Q, 160), 0), 1.0, 0.0).astype(bf16)
    rept = jnp.where(iota((160, Q), 0) // 8 == iota((160, Q), 1), 1.0, 0.0).astype(bf16)
    wide_in = lax.dot_general(win[...], rep, TN, preferred_element_type=f32)
    wide_out = lax.dot_general(wtout[...], rep, TN, preferred_element_type=f32)
    tall_out = jnp.dot(rept, wtout[...], preferred_element_type=f32)
    tall_in = jnp.dot(rept, win[...], preferred_element_type=f32)
    b = jnp.broadcast_to(bias[...], (128, 128)).T
    b = jnp.concatenate([b, b[:, :32]], axis=1)
    high = b.astype(bf16).astype(f32)
    mid = (b - high).astype(bf16).astype(f32)
    low = b - high - mid
    col = iota((128, 160), 1)
    row = iota((160, 128), 0)
    biased = jnp.where(col == 152, high, jnp.where(col == 153, mid, jnp.where(col == 154, low, 0.0)))
    for k in range(8):
        own = (col % 8 == k) & (col < 152)
        own_row = (row % 8 == k) & (row < 152)
        part = slice(k * 128, k * 128 + 128)
        a_in[part, :] = jnp.where(own, wide_in, biased).astype(bf16)
        a_out[part, :] = jnp.where(own, wide_out, 0.0).astype(bf16)
        b_out[:, part] = jnp.where(own_row, tall_out, 0.0).astype(bf16)
        b_in[:, part] = jnp.where(own_row, tall_in, 0.0).astype(bf16)
    for q in range(Q):
        bias_rows[pl.ds(q * 8, 8), :] = jnp.broadcast_to(bias_out[0:1, q : q + 1], (8, 128))


def make_weights(weight_in, weight_out, bias_in, bias_out):
    return pl.pallas_call(
        weights_kernel,
        out_shape=[jax.ShapeDtypeStruct((1024, 160), bf16)] * 2
        + [jax.ShapeDtypeStruct((160, 1024), bf16)] * 2
        + [jax.ShapeDtypeStruct((152, 128), f32)],
        in_specs=vmem(4),
        out_specs=vmem(5),
        cost_estimate=pl.CostEstimate(flops=10**8, bytes_accessed=2 * 10**6, transcendentals=0),
    )(weight_in, weight_out.T, bias_in[None], bias_out[None])


def lines_kernel(dist_low, dist_high, cot_low, cot_high, mask_low, mask_high, up, down, line):
    for out, dist, cot, mask, rows in (
        (up, dist_high, cot_high, mask_high, (6, 7)),
        (down, dist_low, cot_low, mask_low, (0, 1)),
    ):
        for i, r in enumerate(rows):
            line[pl.ds(0, 38), :] = dist[:, r, :]
            line[pl.ds(38, 2), :] = mask[:, r, :].astype(f32)
            line[pl.ds(40, 38), :] = cot[:, r, :]
            line[pl.ds(78, 2), :] = jnp.zeros((2, 128), f32)
            out[pl.ds(i * 80, 80), :] = line[...].astype(bf16)


def outer_lines(dist, cot, mask):
    dist, cot = dist.reshape(38, 128, 128), cot.reshape(38, 128, 128)

    def ends(count):
        return [pl.BlockSpec((count, 8, 128), lambda i: (0, 0, 0)), pl.BlockSpec((count, 8, 128), lambda i: (0, 15, 0))]

    return pl.pallas_call(
        lines_kernel,
        grid=(1,),
        out_shape=[jax.ShapeDtypeStruct((160, 128), bf16)] * 2,
        in_specs=ends(38) + ends(38) + ends(2),
        out_specs=[pl.BlockSpec((160, 128), lambda i: (0, 0))] * 2,
        scratch_shapes=[pltpu.VMEM((80, 128), f32)],
    )(dist, dist, cot, cot, mask, mask)


def pack_kernel(dist, cot, mask, cols):
    lane, row = iota((8, 128), 1), iota((8, 128), 0)
    pick = jnp.zeros((8, 128), f32)
    for j, y in enumerate(COLS):
        pick = jnp.where((row == j) & (lane == y), 1.0, pick)
    pick = pick.astype(bf16)

    def slabs(ref, first, count, place):
        values = ref[pl.ds(first * 128, count * 128), :].astype(f32).astype(bf16)
        got = lax.dot_general(pick, values, NT, preferred_element_type=f32)
        for i in range(count):
            cols[pl.ds(place + i, 8, stride=IDX), :] = got[:, i * 128 : i * 128 + 128]

    for half in range(2):
        slabs(dist, half * 19, 19, half * 19)
        slabs(cot, half * 19, 19, 40 + half * 19)
    slabs(mask, 0, 2, 38)
    for z in range(2):
        cols[pl.ds(78 + z, 8, stride=IDX), :] = jnp.zeros((8, 128), f32)


def pack(dist, cot, mask):
    return pl.pallas_call(
        pack_kernel,
        out_shape=jax.ShapeDtypeStruct((640, 128), f32),
        in_specs=vmem(3),
        out_specs=vmem(1)[0],
        cost_estimate=pl.CostEstimate(flops=10**8, bytes_accessed=6 * 10**6, transcendentals=0),
    )(dist.reshape(38 * 128, 128), cot.reshape(38 * 128, 128), mask.reshape(256, 128))


def corner_kernel(received, cols, send_up, send_down, edge, lines):
    sides = ((2, 0), (3, 1), (0, 126), (1, 127))
    lane = iota((80, 128), 1)
    got = [received[pl.ds(i * 80, 80), :].astype(f32) for i, _ in sides]
    for (_, place), values in zip(sides, got):
        lines[pl.ds(place % 8, 80, stride=8), :] = values
    for r in range(2, 6):
        lines[pl.ds(r, 80, stride=8), :] = jnp.zeros((80, 128), f32)
    for j, y in enumerate(COLS):
        out = jnp.zeros((80, 128), f32)
        for (_, place), values in zip(sides, got):
            out = jnp.where(lane == place, values[:, y : y + 1], out)
        edge[pl.ds(j * 80, 80), :] = out
    for out, first in ((send_up, 0), (send_down, 6)):
        out[:, :128] = cols[pl.ds(first * 80, 160), :].astype(bf16)
        out[:, 128:] = edge[pl.ds(first * 80, 160), :].astype(bf16)


def corners(received, cols):
    return pl.pallas_call(
        corner_kernel,
        out_shape=[jax.ShapeDtypeStruct((160, 256), bf16)] * 2
        + [jax.ShapeDtypeStruct((640, 128), f32)] * 2,
        in_specs=vmem(2),
        out_specs=vmem(4),
    )(received, cols)


def main_kernel(
    dist, cot, mask, cols, edge, beside, lines,
    a_in, a_out, b_out, b_in, bias_out,
    out, parts,
    post, gmid, gpad, hid, hpost, hcot, hmid, strip, spost, smid, flip, uo, acc_in, acc_out, accb,
):
    lane = iota((8, 128), 1)
    row8 = iota((8, 128), 0)

    def join(*parts):
        return jnp.concatenate(parts, axis=1)

    strip[0] = cols[...]
    strip[1] = edge[...]
    strip[0, pl.ds(0, 160), :] = beside[:160, :128].astype(f32)
    strip[1, pl.ds(0, 160), :] = beside[:160, 128:].astype(f32)
    strip[0, pl.ds(480, 160), :] = beside[160:, :128].astype(f32)
    strip[1, pl.ds(480, 160), :] = beside[160:, 128:].astype(f32)

    def strip_of(i):
        return join(strip[0, pl.ds(i, 8, stride=IDX), :], strip[1, pl.ds(i, 8, stride=IDX), :])

    def line_of(i):
        return lines[pl.ds(i * 8, 8), :]

    for q in range(Q):
        for z in range(2):
            i = 2 * q + z
            gpad[q, z, pl.ds(8, 128), :] = cot[q, z]
            halo = line_of(40 + i)
            gpad[q, z, pl.ds(0, 8), :] = halo
            gpad[q, z, pl.ds(136, 8), :] = halo
            gpad[q, z, pl.ds(144, 8), :] = cot[q, z, pl.ds(0, 8), :]

    uo[...] = jnp.zeros_like(uo)
    uo[:, pl.ds(19 * 9, 9), :] = jnp.ones((2 * WIDE, 9, 128), f32)
    acc_in[...] = jnp.zeros_like(acc_in)
    acc_out[...] = jnp.zeros_like(acc_out)
    accb[...] = jnp.zeros_like(accb)
    flip[...] = jnp.zeros_like(flip)

    def operand(values):
        ones = jnp.ones(values[0].shape, f32)
        return jnp.concatenate(values + [ones], axis=0).astype(bf16)

    def hidden(values):
        return jnp.tanh(jnp.dot(a_in[...], operand(values), preferred_element_type=f32))

    def collide(d, solid, keep):
        t = hidden(d)
        if keep is not None:
            hid[keep] = t
        o = jnp.dot(b_out[...], t.astype(bf16), preferred_element_type=f32)
        res = []
        for q in range(Q):
            bias = bias_out[pl.ds(q * 8, 8), :]
            val = d[q] + o[q * 8 : q * 8 + 8] + join(*[bias] * (d[q].shape[1] // 128))
            val = jnp.where(solid, d[OPP[q]], val)
            res.append(val.astype(bf16).astype(f32))
        return res

    def backward(u, g, solid, t, partial):
        og = [jnp.where(solid, 0.0, v) for v in g]
        if t is None:
            t = hidden(u)
        hg = jnp.dot(a_out[...], operand(og), preferred_element_type=f32)
        hb = (hg * (1.0 - t * t)).astype(bf16)
        ig = jnp.dot(b_in[...], hb, preferred_element_type=f32)
        if partial:
            act = t.astype(bf16)
            halves = [slice(h * 128, h * 128 + 128) for h in range(2 * WIDE)]
            for q in range(Q):
                for h, part in enumerate(halves):
                    uo[h, pl.ds(q * 9, 8), :] = u[q][:, part]
                    uo[h, pl.ds(216 + q * 9, 8), :] = og[q][:, part]
                accb[pl.ds(q * 8, 8), :] += sum(og[q][:, part] for part in halves)

            def cells(first):
                lines24 = join(
                    *[uo[h, pl.ds(first + k, 24, stride=9), :] for k in range(8) for h in range(2 * WIDE)]
                )
                return jnp.concatenate([lines24, jnp.zeros((8, lines24.shape[1]), f32)], axis=0).astype(bf16)

            def units(values):
                return join(*[values[k * 128 : k * 128 + 128] for k in range(8)])

            left = jnp.concatenate([units(hb), cells(216)], axis=0)
            right = jnp.concatenate([units(act), cells(0)], axis=0)
            both = lax.dot_general(left, right, NT, preferred_element_type=f32)
            acc_in[:, :32] += both[:128, 128:]
            acc_out[...] += both[128:, :128]
        return [
            og[q] + ig[q * 8 : q * 8 + 8] + jnp.where(solid, g[OPP[q]], 0.0) for q in range(Q)
        ]

    def streamed(ref, halo, rows, orient):
        res = []
        for q in range(Q):
            cx, cy, cz = (orient * c for c in VEL[q])
            pieces = []
            for row in rows:
                for z in range(2):
                    zs = (z - cz) % 2
                    v = ref[q, zs, pl.ds(row - cx, 8), :]
                    if cy:
                        k = PLACE[q] * 2 + zs
                        h = halo[pl.ds(row - cx, 8), :][:, k : k + 1]
                        v = pltpu.roll(v, 1 if cy == 1 else 127, 1)
                        v = jnp.where(lane == (0 if cy == 1 else 127), h, v)
                    pieces.append(v)
            res.append(join(*pieces))
        return res

    def streamed_strip(get, orient, z):
        res = []
        for q in range(Q):
            cx, cy, cz = (orient * c for c in VEL[q])
            v = get(q, (z - cz) % 2)
            if cy:
                v = pltpu.roll(v, cy % 8, 0)
            if cx:
                v = pltpu.roll(v, cx % 256, 1)
            res.append(v)
        return res

    def to_halo(get, halo, orient):
        for q in SIDE:
            j = 1 if orient * VEL[q][1] == 1 else 6
            for z in range(2):
                flip[pl.ds(PLACE[q] * 2 + z, 1), :] = get(q, z, j)
        low = flip[:, :128].T
        high = flip[:, 128:].T
        halo[pl.ds(8, 128), :] = low
        outer = jnp.where(row8 < 4, high[0:8], high[120:128])
        halo[pl.ds(136, 8), :] = outer
        halo[pl.ds(0, 8), :] = outer
        halo[pl.ds(144, 8), :] = low[0:8]

    def put(ref, rows, values):
        for q in range(Q):
            for i, row in enumerate(rows):
                for z in range(2):
                    at = i * 256 + z * 128
                    ref[q, z, pl.ds(row, 8), :] = values[q][:, at : at + 128]

    def put_outer(ref, side, values):
        for q in range(Q):
            for z in range(2):
                ref[q, z, pl.ds(136, 8), :] = values[q][:, z * 128 : z * 128 + 128]
                ref[q, z, pl.ds(0, 8), :] = values[q][:, z * 128 : z * 128 + 128]
                ref[q, z, pl.ds(144, 8), :] = ref[q, z, pl.ds(8, 8), :]
                side[z, q] = values[q][:, 256 + z * 256 : 512 + z * 256]

    def block(ref, rows):
        return [join(*[ref[q, z, pl.ds(r, 8), :] for r in rows for z in range(2)]) for q in range(Q)]

    def solid_at(rows):
        return join(*[mask[z, pl.ds(r, 8), :] for r in rows for z in range(2)]) > 0

    outer_solid = join(line_of(38), line_of(39), strip_of(38), strip_of(39)) > 0.5

    def rows_of(b, offset):
        return [pl.multiple_of((b + w * STEPS) * 8, 8) + offset for w in range(WIDE)]

    def first(b, carry):
        put(post, rows_of(b, 8), collide(block(dist, rows_of(b, 0)), solid_at(rows_of(b, 0)), b))
        return carry

    lax.fori_loop(0, STEPS, first, 0)
    d = [
        join(line_of(2 * q), line_of(2 * q + 1), strip_of(2 * q), strip_of(2 * q + 1)) for q in range(Q)
    ]
    put_outer(post, spost, collide(d, outer_solid, None))
    to_halo(lambda q, z, j: spost[z, q, pl.ds(j, 1), :], hpost, 1)
    to_halo(
        lambda q, z, j: join(
            strip[0, pl.ds(j * IDX + 40 + 2 * q + z, 1), :], strip[1, pl.ds(j * IDX + 40 + 2 * q + z, 1), :]
        ),
        hcot,
        -1,
    )

    def second(b, carry):
        u = streamed(post, hpost, rows_of(b, 8), 1)
        g = streamed(gpad, hcot, rows_of(b, 8), -1)
        put(gmid, rows_of(b, 8), backward(u, g, solid_at(rows_of(b, 0)), None, True))
        return carry

    lax.fori_loop(0, STEPS, second, 0)
    us = [streamed(post, hpost, [136], 1)] + [
        streamed_strip(lambda q, zs: spost[zs, q], 1, z) for z in range(2)
    ]
    gs = [streamed(gpad, hcot, [136], -1)] + [
        streamed_strip(lambda q, zs: strip_of(40 + 2 * q + zs), -1, z) for z in range(2)
    ]
    u = [join(*[v[q] for v in us]) for q in range(Q)]
    g = [join(*[v[q] for v in gs]) for q in range(Q)]
    put_outer(gmid, smid, backward(u, g, outer_solid, None, False))
    to_halo(lambda q, z, j: smid[z, q, pl.ds(j, 1), :], hmid, -1)

    def third(b, carry):
        g = streamed(gmid, hmid, rows_of(b, 8), -1)
        rows = rows_of(b, 0)
        put(out, rows, backward(block(dist, rows), g, solid_at(rows), hid[b], True))
        return carry

    lax.fori_loop(0, STEPS, third, 0)
    parts[pl.ds(0, 20), :] = acc_in[...].T[:20]
    parts[pl.ds(20, 20), :] = acc_out[pl.ds(0, 20), :]
    flip[...] = jnp.zeros_like(flip)
    for q in range(Q):
        flip[pl.ds(q, 1), :128] = jnp.sum(accb[pl.ds(q * 8, 8), :], axis=0, keepdims=True)
    parts[pl.ds(40, 8), :] = jnp.broadcast_to(jnp.sum(flip[:, :128].T, axis=0, keepdims=True), (8, 128))


def main_call(*args):
    field = pltpu.VMEM((Q, 2, 152, 128), f32)
    halo = pltpu.VMEM((152, 128), f32)
    return pl.pallas_call(
        main_kernel,
        out_shape=[jax.ShapeDtypeStruct((Q, 2, 128, 128), f32), jax.ShapeDtypeStruct((48, 128), f32)],
        in_specs=vmem(len(args)),
        out_specs=vmem(2),
        scratch_shapes=[
            field, field, field,
            pltpu.VMEM((STEPS, 1024, 256 * WIDE), f32),
            halo, halo, halo,
            pltpu.VMEM((2, 640, 128), f32),
            pltpu.VMEM((2, Q, 8, 256), f32),
            pltpu.VMEM((2, Q, 8, 256), f32),
            pltpu.VMEM((128, 256), f32),
            pltpu.VMEM((2 * WIDE, 432, 128), f32),
            pltpu.VMEM((128, 128), f32),
            pltpu.VMEM((32, 128), f32),
            pltpu.VMEM((152, 128), f32),
        ],
        compiler_params=pltpu.CompilerParams(vmem_limit_bytes=58 * 2**20),
    )(*args)


def neighbours(axis):
    size = lax.axis_size(axis)
    up = [(i, (i + 1) % size) for i in range(size)]
    return up, [(j, i) for i, j in up]


def summed(values):
    nx, ny = lax.axis_size("gx"), lax.axis_size("gy")
    if (nx, ny) == (8, 16):
        stages = (((0, 1), (1, 0), (0, 2)), ((2, 0), (4, 0)), ((0, 4), (0, 8)))
    else:
        stages = [((1 << k, 0),) for k in range(nx.bit_length() - 1)]
        stages += [((0, 1 << k),) for k in range(ny.bit_length() - 1)]
    for bits in stages:
        got = [values]
        for d in range(1, 1 << len(bits)):
            fx = sum(bx for k, (bx, _) in enumerate(bits) if d >> k & 1)
            fy = sum(by for k, (_, by) in enumerate(bits) if d >> k & 1)
            pairs = [(x * ny + y, (x ^ fx) * ny + (y ^ fy)) for x in range(nx) for y in range(ny)]
            got.append(lax.ppermute(values, ("gx", "gy"), pairs))
        while len(got) > 1:
            got = [got[i] + got[i + 1] for i in range(0, len(got), 2)]
        values = got[0]
    return values


def shards(dist, cot, mask, weight_in, bias_in, weight_out, bias_out):
    send_up, send_down = outer_lines(dist, cot, mask)
    up, down = neighbours("gx")
    from_up = lax.ppermute(send_up, "gx", up)
    from_down = lax.ppermute(send_down, "gx", down)
    cols = pack(dist, cot, mask)
    side_up, side_down, edge, lines = corners(jnp.concatenate([from_up, from_down]), cols)
    up, down = neighbours("gy")
    from_left = lax.ppermute(side_up, "gy", up)
    from_right = lax.ppermute(side_down, "gy", down)
    weight_in, _ = lax.optimization_barrier((weight_in, edge))
    nets = make_weights(weight_in, weight_out, bias_in, bias_out)
    grad, parts = main_call(
        dist, cot, mask, cols, edge, jnp.concatenate([from_left, from_right]), lines, *nets
    )
    total = summed(parts)
    cells = mask.size * lax.axis_size("gx") * lax.axis_size("gy")
    total = total * (1.0 / math.sqrt(cells))
    return grad, total[:19], total[19], total[20:39].T, total[40, :19]


def solution(mesh):
    field = P(None, None, "gx", "gy")
    return jax.shard_map(
        shards,
        mesh=mesh,
        in_specs=(field, field, P(None, "gx", "gy"), P(), P(), P(), P()),
        out_specs=(field, P(), P(), P(), P()),
        check_vma=False,
    )
```
